128 devices in a mesh: row: 16 (over y, z), col: 8 (over x, core).
Axes of the slice: x: 4, y: 4, z: 4, core: 2. Of those that a mesh axis runs over, the one named last changes fastest.
Arguments:
- tokens: bfloat16 [256, 12288], P('row', 'col'), may hold values from -6 to 6
- out_grad: bfloat16 [256, 12288], P('row', 'col'), may hold values from -2 to 2
- w1_blocks: bfloat16 [23040, 128, 128], P(('row', 'col')), may hold values from -0.078125 to 0.078125
- w1_index: int32 [23040, 2], P(('row', 'col')), may hold values from 0 to 24, as said below
- w2_blocks: bfloat16 [23040, 128, 128], P(('row', 'col')), may hold values from -0.0390625 to 0.0390625
- w2_index: int32 [23040, 2], P(('row', 'col')), may hold values from 0 to 23, as said below
Outputs:
- output: bfloat16 [256, 12288], P('row', 'col')
- grad_input: bfloat16 [256, 12288], P('row', 'col')
- grad_w1: bfloat16 [23040, 128, 128], P(('row', 'col'))
- grad_w2: bfloat16 [23040, 128, 128], P(('row', 'col'))
The draws below stay inside these ranges and needn't reach their ends.
Inputs may be any that keep to these rules, and one draw needn't show every extreme that they name: `w1_index`: within each tile's 180 slots the filled ones name distinct blocks of the tile; a slot with column 24 is empty and its row is any block row; in every draw some tile fills all 180 slots and some tile fills 180 // 2 of them. `w2_index`: within each tile's 180 slots the filled ones name distinct blocks of the tile; a slot with column 12 is empty and its row is any block row; in every draw some tile fills all 180 slots and some tile fills 180 // 2 of them.
All inputs are finite; a program needn't handle non-finite values.
Results may differ from the reference program's by a relative error of at most 0.03.
Values may be sent and summed in bfloat16 or wider, within the bound.
A program may use at most 256 MiB of HBM per device.

```python
import jax
import jax.numpy as jnp
from jax import lax

D = 12288
FF = 49152
BLK = 128
TOKENS = 256
BR = 12
BC = 24
CAP = 180
N_COL = 8
DEVICES = 128


def slot_table(key, row_count, col_count):
    full_key, lean_key, count_key, perm_key = jax.random.split(key, 4)
    fullest = jax.random.randint(full_key, (), 0, DEVICES)
    leanest = (fullest + 1 + jax.random.randint(lean_key, (), 0, DEVICES - 1)) % DEVICES
    counts = jax.random.randint(count_key, (DEVICES,), CAP // 2, CAP + 1)
    places = jnp.arange(DEVICES)
    counts = jnp.where(places == fullest, CAP, counts)
    counts = jnp.where(places == leanest, CAP // 2, counts)
    perms = jax.vmap(lambda sub: jax.random.permutation(sub, row_count * col_count)[:CAP])(jax.random.split(perm_key, DEVICES))
    filled = jnp.arange(CAP)[None, :] < counts[:, None]
    rows = perms // col_count
    cols = jnp.where(filled, perms % col_count, col_count)
    return jnp.stack([rows, cols], -1).reshape(DEVICES * CAP, 2).astype(jnp.int32)


def draw_w1_index(key, part):
    key = jax.random.fold_in(key, 11)
    return slot_table(key, BR, BC)


def draw_w2_index(key, part):
    key = jax.random.fold_in(key, 23)
    return slot_table(key, BC, BR)


def steps_of(key, extent, pieces, low, high):
    def one(position, blocks):
        steps = jax.random.uniform(jax.random.fold_in(jax.random.fold_in(key, 6), position), (blocks,), jnp.float32, low / len(pieces), high / len(pieces))
        return jnp.repeat(jnp.exp(steps), extent[position] // blocks).reshape((-1,) + (1,) * (len(extent) - position - 1))

    level = one(*pieces[0])
    for cut in pieces[1:]:
        level = level * one(*cut)
    return level


def bell_draw(stream_key, extent, scale, most, cuts=(), kind=jnp.bfloat16):
    values = scale * jax.random.normal(stream_key, extent, jnp.float32)
    if cuts:
        values = values * steps_of(stream_key, extent, cuts, -0.22, 0.18)
    return jnp.clip(values, -most, most).astype(kind)


def setup_inputs(seed: int = 0) -> dict:
    arg_keys = jax.random.split(jax.random.key(seed), 7)
    return {
        "tokens": bell_draw(arg_keys[0], (TOKENS, D), 1.0, 6.0, ((0, 16), (1, 8))),
        "out_grad": bell_draw(arg_keys[1], (TOKENS, D), 0.3, 2.0, ((0, 16), (1, 8))),
        "w1_blocks": bell_draw(arg_keys[2], (DEVICES * CAP, BLK, BLK), (D // 2) ** -0.5, 0.078125, ((0, 128),)),
        "w1_index": draw_w1_index(jax.random.fold_in(arg_keys[6], 71), 0),
        "w2_blocks": bell_draw(arg_keys[4], (DEVICES * CAP, BLK, BLK), (FF // 2) ** -0.5, 0.0390625, ((0, 128),)),
        "w2_index": draw_w2_index(jax.random.fold_in(arg_keys[6], 71), 0),
    }


def gelu_pair(value):
    cubic_term = 0.044715 * value * value * value
    tangent = jnp.tanh(0.7978845608 * (value + cubic_term))
    result = 0.5 * value * (1.0 + tangent)
    derivative = 0.5 * (1.0 + tangent) + 0.5 * value * (1.0 - tangent * tangent) * 0.7978845608 * (1.0 + 3.0 * 0.044715 * value * value)
    return result, derivative


def dense_tile(blocks, index, row_count, col_count):
    filled = index[:, 1] < col_count
    target = jnp.where(filled, index[:, 0] * col_count + index[:, 1], row_count * col_count).astype(jnp.int32)
    holder = jnp.zeros((row_count * col_count + 1, BLK, BLK), blocks.dtype).at[target].set(blocks)
    holder = holder[: row_count * col_count]
    return holder.reshape(row_count, col_count, BLK, BLK).transpose(0, 2, 1, 3).reshape(row_count * BLK, col_count * BLK)


def slot_blocks(dense, index, row_count, col_count):
    filled = index[:, 1] < col_count
    target = jnp.where(filled, index[:, 0] * col_count + index[:, 1], 0).astype(jnp.int32)
    holder = dense.reshape(row_count, BLK, col_count, BLK).transpose(0, 2, 1, 3).reshape(row_count * col_count, BLK, BLK)
    return jnp.where(filled[:, None, None], holder[target], 0.0)


def rounded(value):
    return lax.optimization_barrier(value.astype(jnp.bfloat16)).astype(jnp.float32)


def reference(tokens, out_grad, w1_blocks, w1_index, w2_blocks, w2_index):
    feat_tile = BR * BLK
    unit_tile = BC * BLK
    first_blocks = w1_blocks.reshape(DEVICES, CAP, BLK, BLK)
    first_index = w1_index.reshape(DEVICES, CAP, 2)
    second_blocks = w2_blocks.reshape(DEVICES, CAP, BLK, BLK)
    second_index = w2_index.reshape(DEVICES, CAP, 2)
    devices = jnp.arange(DEVICES, dtype=jnp.int32)

    def forward_step(carry, items):
        hidden, hidden_grad = carry
        device, blocks_one, index_one, blocks_two, index_two = items
        row_pos = device // N_COL
        col_pos = device % N_COL
        inputs = lax.dynamic_slice_in_dim(tokens, col_pos * feat_tile, feat_tile, 1)
        grads = lax.dynamic_slice_in_dim(out_grad, col_pos * feat_tile, feat_tile, 1)
        tile_one = dense_tile(blocks_one, index_one, BR, BC)
        tile_two = dense_tile(blocks_two, index_two, BC, BR)
        part_hidden = rounded(jnp.dot(inputs, tile_one, preferred_element_type=jnp.float32))
        part_grad = rounded(jnp.dot(grads, tile_two.T, preferred_element_type=jnp.float32))
        start = row_pos * unit_tile
        hidden = lax.dynamic_update_slice_in_dim(hidden, lax.dynamic_slice_in_dim(hidden, start, unit_tile, 1) + part_hidden, start, 1)
        hidden_grad = lax.dynamic_update_slice_in_dim(hidden_grad, lax.dynamic_slice_in_dim(hidden_grad, start, unit_tile, 1) + part_grad, start, 1)
        return (hidden, hidden_grad), None

    zeros_hidden = jnp.zeros((TOKENS, FF), jnp.float32)
    (hidden, hidden_grad), unused = lax.scan(forward_step, (zeros_hidden, zeros_hidden), (devices, first_blocks, first_index, second_blocks, second_index))
    activated_f, derivative = gelu_pair(hidden)
    activated = activated_f.astype(jnp.bfloat16)
    pre_grad = (hidden_grad * derivative).astype(jnp.bfloat16)

    def backward_step(carry, items):
        output, grad_input = carry
        device, blocks_one, index_one, blocks_two, index_two = items
        row_pos = device // N_COL
        col_pos = device % N_COL
        inputs = lax.dynamic_slice_in_dim(tokens, col_pos * feat_tile, feat_tile, 1)
        grads = lax.dynamic_slice_in_dim(out_grad, col_pos * feat_tile, feat_tile, 1)
        acts = lax.dynamic_slice_in_dim(activated, row_pos * unit_tile, unit_tile, 1)
        pres = lax.dynamic_slice_in_dim(pre_grad, row_pos * unit_tile, unit_tile, 1)
        tile_one = dense_tile(blocks_one, index_one, BR, BC)
        tile_two = dense_tile(blocks_two, index_two, BC, BR)
        part_out = rounded(jnp.dot(acts, tile_two, preferred_element_type=jnp.float32))
        part_in = rounded(jnp.dot(pres, tile_one.T, preferred_element_type=jnp.float32))
        start = col_pos * feat_tile
        output = lax.dynamic_update_slice_in_dim(output, lax.dynamic_slice_in_dim(output, start, feat_tile, 1) + part_out, start, 1)
        grad_input = lax.dynamic_update_slice_in_dim(grad_input, lax.dynamic_slice_in_dim(grad_input, start, feat_tile, 1) + part_in, start, 1)
        slots_one = slot_blocks(jnp.dot(inputs.T, pres, preferred_element_type=jnp.float32), index_one, BR, BC).astype(jnp.bfloat16)
        slots_two = slot_blocks(jnp.dot(acts.T, grads, preferred_element_type=jnp.float32), index_two, BC, BR).astype(jnp.bfloat16)
        return (output, grad_input), (slots_one, slots_two)

    zeros_out = jnp.zeros((TOKENS, D), jnp.float32)
    (output, grad_input), (grad_one, grad_two) = lax.scan(backward_step, (zeros_out, zeros_out), (devices, first_blocks, first_index, second_blocks, second_index))
    return (output.astype(jnp.bfloat16), grad_input.astype(jnp.bfloat16), grad_one.reshape(DEVICES * CAP, BLK, BLK), grad_two.reshape(DEVICES * CAP, BLK, BLK))
```

```python
import functools

import jax
import jax.numpy as jnp
from jax import lax
from jax.experimental import pallas as pl
from jax.experimental.pallas import tpu as pltpu
from jax.sharding import PartitionSpec as P

MESH = pl.DeviceIdType.MESH
BLK = 128
CAP = 180
FB = 12
UB = 24
FT = FB * BLK
UT = UB * BLK
TOK = 256
ITEMS = 4
NU = UT // ITEMS
F32 = jnp.float32
BF16 = jnp.bfloat16
NT = (((1,), (1,)), ((), ()))


def gelu_pair(value):
    cubic_term = 0.044715 * value * value * value
    tangent = jnp.tanh(0.7978845608 * (value + cubic_term))
    result = 0.5 * value * (1.0 + tangent)
    derivative = 0.5 * (1.0 + tangent) + 0.5 * value * (1.0 - tangent * tangent) * 0.7978845608 * (
        1.0 + 3.0 * 0.044715 * value * value
    )
    return (result, derivative)


def fused_kernel(
    n_sems,
    tok_ref,
    grad_ref,
    inv1_ref,
    inv2_ref,
    w1_hbm,
    w2_hbm,
    out_ref,
    gin_ref,
    tokall_hbm,
    gall_hbm,
    ag_hbm,
    w1v,
    w2v,
    dense1,
    dense2,
    tok_all,
    g_all,
    part,
    rc,
    m1l,
    m1r,
    m2l,
    m2r,
    ag,
    acc_o,
    acc_i,
    po,
    pi,
    c1o,
    c1i,
    c2o,
    c2i,
    send_sems,
    recv_sems,
    local_sems,
):
    row = lax.axis_index("row")
    col = lax.axis_index("col")
    y, z = row // 4, row % 4
    x, k = col // 2, col % 2
    yr, yl, yo = (y + 1) % 4, (y + 3) % 4, (y + 2) % 4
    zr, zl, zo = (z + 1) % 4, (z + 3) % 4, (z + 2) % 4
    xr, xl, xo = (x + 1) % 4, (x + 3) % 4, (x + 2) % 4
    sib = (row, x * 2 + 1 - k)
    dev_xr, dev_xl = (row, xr * 2 + k), (row, xl * 2 + k)
    dev_yr, dev_yl = (yr * 4 + z, col), (yl * 4 + z, col)
    dev_zr, dev_zl = (y * 4 + zr, col), (y * 4 + zl, col)

    load1 = pltpu.make_async_copy(w1_hbm, w1v.at[pl.ds(0, CAP)], local_sems.at[0])
    load2 = pltpu.make_async_copy(w2_hbm, w2v.at[pl.ds(0, CAP)], local_sems.at[1])
    load1.start()
    load2.start()

    barrier = pltpu.get_barrier_semaphore()
    for dev in (sib, dev_xr, dev_xl, dev_yr, dev_yl, dev_zr, dev_zl):
        pl.semaphore_signal(barrier, inc=1, device_id=dev, device_id_type=MESH)
    pl.semaphore_wait(barrier, 7)

    started = []

    def send(src, dst, dev):
        n = len(started)
        copy = pltpu.make_async_remote_copy(
            src_ref=src,
            dst_ref=dst,
            send_sem=send_sems.at[n],
            recv_sem=recv_sems.at[n],
            device_id=dev,
            device_id_type=MESH,
        )
        copy.start()
        started.append(copy)
        return copy

    w1v[CAP] = jnp.zeros((BLK, BLK), BF16)
    w2v[CAP] = jnp.zeros((BLK, BLK), BF16)
    tok_all[y, z] = tok_ref[...]
    g_all[y, z] = grad_ref[...]

    def put(ref, i, j, dev):
        return send(ref.at[i, j], ref.at[i, j], dev)

    def put_half(ref, i, j, half, dev):
        view = ref.at[i, j, :, pl.ds(half * (FT // 2), FT // 2)]
        return send(view, view, dev)

    t_r, t_l = put(tok_all, y, z, dev_zr), put(tok_all, y, z, dev_zl)
    g_r, g_l = put(g_all, y, z, dev_yr), put(g_all, y, z, dev_yl)
    tb = [(put(tok_all, y, z, dev_yr), put(tok_all, y, z, dev_yl))]
    gb = [(put(g_all, y, z, dev_zr), put(g_all, y, z, dev_zl))]
    t_r.wait_recv()
    t_fr = put_half(tok_all, y, zl, 0, dev_zr)
    t_l.wait_recv()
    t_fl = put_half(tok_all, y, zr, 1, dev_zl)
    g_r.wait_recv()
    g_fr = put_half(g_all, yl, z, 0, dev_yr)
    g_l.wait_recv()
    g_fl = put_half(g_all, yr, z, 1, dev_yl)
    tb.append((put(tok_all, y, zl, dev_yr), put(tok_all, y, zl, dev_yl)))
    gb.append((put(g_all, yl, z, dev_zr), put(g_all, yl, z, dev_zl)))
    tb.append((put(tok_all, y, zr, dev_yr), put(tok_all, y, zr, dev_yl)))
    gb.append((put(g_all, yr, z, dev_zr), put(g_all, yr, z, dev_zl)))

    load1.wait()

    def fill1(i, carry):
        for j in range(UB):
            dense1[pl.ds(pl.multiple_of(i * BLK, BLK), BLK), pl.ds(j * BLK, BLK)] = w1v[inv1_ref[i * UB + j]]
        return carry

    def fill2(i, carry):
        for j in range(FB):
            dense2[pl.ds(pl.multiple_of(i * BLK, BLK), BLK), pl.ds(j * BLK, BLK)] = w2v[inv2_ref[i * FB + j]]
        return carry

    lax.fori_loop(0, FB, fill1, 0)

    t_fr.wait_recv()
    t_fl.wait_recv()
    tb.append((put(tok_all, y, zo, dev_yr), put(tok_all, y, zo, dev_yl)))
    g_fr.wait_recv()
    g_fl.wait_recv()
    gb.append((put(g_all, yo, z, dev_zr), put(g_all, yo, z, dev_zl)))

    tb[0][0].wait_recv()
    t_f = [put(tok_all, yl, z, dev_yr)]
    gb[0][0].wait_recv()
    g_f = [put(g_all, y, zl, dev_zr)]
    load2.wait()
    lax.fori_loop(0, UB, fill2, 0)
    tb[1][0].wait_recv()
    t_f.append(put(tok_all, yl, zl, dev_yr))
    gb[1][0].wait_recv()
    g_f.append(put(g_all, yl, zl, dev_zr))
    tb[2][1].wait_recv()
    t_f.append(put(tok_all, yr, zr, dev_yl))
    gb[2][1].wait_recv()
    g_f.append(put(g_all, yr, zr, dev_zl))
    tb[3][1].wait_recv()
    t_f.append(put(tok_all, yr, zo, dev_yl))
    gb[3][1].wait_recv()
    g_f.append(put(g_all, yo, zr, dev_zl))
    for pair in (tb, gb):
        pair[0][1].wait_recv()
        pair[1][1].wait_recv()
        pair[2][0].wait_recv()
        pair[3][0].wait_recv()
    for copy in t_f + g_f:
        copy.wait_recv()

    save_t = pltpu.make_async_copy(tok_all, tokall_hbm, local_sems.at[2])
    save_g = pltpu.make_async_copy(g_all, gall_hbm, local_sems.at[3])
    save_t.start()
    save_g.start()

    TN = 256

    def forward(u):
        def tile(n, carry):
            here = pl.ds(pl.multiple_of(n * TN, TN), TN)
            units = pl.ds(pl.multiple_of(u * NU + n * TN, TN), TN)
            tokens = tok_all[...].reshape(TOK, FT)
            grads = g_all[...].reshape(TOK, FT)
            hidden = jnp.dot(tokens, dense1[:, units], preferred_element_type=F32)
            part[u, :, :, 0, :, here] = hidden.astype(BF16).reshape(2, 4, 32, TN)
            hgrad = lax.dot_general(grads, dense2[units, :], NT, preferred_element_type=F32)
            part[u, :, :, 1, :, here] = hgrad.astype(BF16).reshape(2, 4, 32, TN)
            return carry

        lax.fori_loop(0, NU // TN, tile, 0)

    def backward(u):
        base = pl.ds(u * NU, NU)

        def tile(n, carry):
            here = pl.ds(pl.multiple_of(n * TN, TN), TN)
            act = ag[u, :, :, 0].reshape(TOK, NU)
            pre = ag[u, :, :, 1].reshape(TOK, NU)
            o = jnp.dot(act, dense2[base, here], preferred_element_type=F32)
            i = lax.dot_general(pre, dense1[here, base], NT, preferred_element_type=F32)
            if u > 0:
                o = o + acc_o[:, here]
                i = i + acc_i[:, here]
            if u < ITEMS - 1:
                acc_o[:, here] = o
                acc_i[:, here] = i
            else:
                po[:, :, :, here] = o.astype(BF16).reshape(4, 4, 16, TN)
                pi[:, :, :, here] = i.astype(BF16).reshape(4, 4, 16, TN)
            return carry

        lax.fori_loop(0, FT // TN, tile, 0)

    flight = [dict() for _ in range(ITEMS)]

    def add(a, b):
        return (a.astype(F32) + b.astype(F32)).astype(BF16)

    def stage0(u):
        forward(u)
        flight[u]["core"] = send(part.at[u, 1 - k], rc.at[u], sib)

    def stage1(u):
        f = flight[u]
        f["core"].wait_recv()
        for where in (xo, xr, xl, x):
            part[u, k, where] = add(part[u, k, where], rc[u, where])
        f["lh"] = send(part.at[u, k, xo, 0], m1l.at[u, 0], dev_xr)
        f["rg"] = send(part.at[u, k, xo, 1], m1r.at[u, 1], dev_xl)
        f["lg"] = send(part.at[u, k, xr, 1], m1l.at[u, 1], dev_xr)
        f["rh"] = send(part.at[u, k, xl, 0], m1r.at[u, 0], dev_xl)

    def stage2(u):
        f = flight[u]
        f["lh"].wait_recv()
        part[u, k, xr, 0] = add(part[u, k, xr, 0], m1l[u, 0])
        f["l2"] = send(part.at[u, k, xr, 0], m2l.at[u], dev_xr)
        f["rg"].wait_recv()
        part[u, k, xl, 1] = add(part[u, k, xl, 1], m1r[u, 1])
        f["r2"] = send(part.at[u, k, xl, 1], m2r.at[u], dev_xl)

    def stage3(u):
        f = flight[u]
        for name in ("lg", "rh", "l2", "r2"):
            f[name].wait_recv()
        hidden = part[u, k, x, 0].astype(F32) + m1r[u, 0].astype(F32) + m2l[u].astype(F32)
        hgrad = part[u, k, x, 1].astype(F32) + m1l[u, 1].astype(F32) + m2r[u].astype(F32)
        act, slope = gelu_pair(hidden)
        ag[u, k, x, 0] = act.astype(BF16)
        ag[u, k, x, 1] = (hgrad * slope).astype(BF16)
        mine = ag.at[u, k, x]
        f["ar"] = send(mine, mine, dev_xr)
        f["al"] = send(mine, mine, dev_xl)
        f["s0"] = send(mine, mine, sib)

    def stage4(u):
        f = flight[u]
        f["ar"].wait_recv()
        f["fr"] = send(ag.at[u, k, xl, 0], ag.at[u, k, xl, 0], dev_xr)
        f["s1"] = send(ag.at[u, k, xl], ag.at[u, k, xl], sib)
        f["al"].wait_recv()
        f["fl"] = send(ag.at[u, k, xr, 1], ag.at[u, k, xr, 1], dev_xl)
        f["s2"] = send(ag.at[u, k, xr], ag.at[u, k, xr], sib)

    def stage5(u):
        f = flight[u]
        f["fr"].wait_recv()
        f["fl"].wait_recv()
        f["s3"] = send(ag.at[u, k, xo], ag.at[u, k, xo], sib)

    def stage6(u):
        f = flight[u]
        for name in ("s0", "s1", "s2", "s3"):
            f[name].wait_recv()
        backward(u)

    stages = (stage0, stage1, stage2, stage3, stage4, stage5, stage6)
    for t in range(ITEMS + 6):
        for s in (5, 4, 3, 2, 1, 0, 6):
            if 0 <= t - s < ITEMS:
                stages[s](t - s)

    save_a = pltpu.make_async_copy(ag, ag_hbm, local_sems.at[4])
    save_a.start()

    def ring(block, land, here, right, left, opposite, dev_r, dev_l, halves):
        one, two = halves
        f = {}
        f["l1"] = send(block(opposite, one), land.at[0], dev_r)
        f["r2"] = send(block(opposite, two), land.at[3], dev_l)
        f["l2"] = send(block(right, two), land.at[1], dev_r)
        f["r1"] = send(block(left, one), land.at[2], dev_l)

        def middle():
            f["l1"].wait_recv()
            spot = block(right, one)
            spot[...] = add(spot[...], land[0])
            f["l3"] = send(spot, land.at[4], dev_r)
            f["r2"].wait_recv()
            spot = block(left, two)
            spot[...] = add(spot[...], land[3])
            f["r3"] = send(spot, land.at[5], dev_l)

        def final():
            for name in ("l2", "r1", "l3", "r3"):
                f[name].wait_recv()
            first = block(here, one)[...].astype(F32) + land[2].astype(F32) + land[4].astype(F32)
            second = block(here, two)[...].astype(F32) + land[1].astype(F32) + land[5].astype(F32)
            return first, second

        return middle, final

    pair = (pl.ds(0, 2), pl.ds(2, 2))
    lanes = (pl.ds(0, FT // 2), pl.ds(FT // 2, FT // 2))
    o_mid, o_fin = ring(lambda p, h: po.at[p, h], c1o, y, yr, yl, yo, dev_yr, dev_yl, pair)
    i_mid, i_fin = ring(lambda p, h: pi.at[h, p], c1i, z, zr, zl, zo, dev_zr, dev_zl, pair)
    o_mid()
    i_mid()
    first, second = o_fin()
    po[y, pair[0]] = first.astype(BF16)
    po[y, pair[1]] = second.astype(BF16)
    o_mid, o_fin = ring(lambda p, h: po.at[y, p, :, h], c2o, z, zr, zl, zo, dev_zr, dev_zl, lanes)
    first, second = i_fin()
    pi[pair[0], z] = first.astype(BF16)
    pi[pair[1], z] = second.astype(BF16)
    i_mid, i_fin = ring(lambda p, h: pi.at[p, z, :, h], c2i, y, yr, yl, yo, dev_yr, dev_yl, lanes)
    o_mid()
    i_mid()
    first, second = o_fin()
    out_ref[:, lanes[0]] = first.astype(BF16)
    out_ref[:, lanes[1]] = second.astype(BF16)
    first, second = i_fin()
    gin_ref[:, lanes[0]] = first.astype(BF16)
    gin_ref[:, lanes[1]] = second.astype(BF16)

    for copy in started:
        copy.wait_send()
    save_t.wait()
    save_g.wait()
    save_a.wait()
    assert len(started) == n_sems, len(started)


N_SEMS = 32 + 15 * ITEMS + 24


def fused(tokens, out_grad, inv1, inv2, w1, w2):
    vmem = pl.BlockSpec(memory_space=pltpu.VMEM)
    smem = pl.BlockSpec(memory_space=pltpu.SMEM)
    hbm = pl.BlockSpec(memory_space=pl.ANY)
    flops = 4 * 2 * TOK * FT * UT
    return pl.pallas_call(
        functools.partial(fused_kernel, N_SEMS),
        out_shape=(
            jax.ShapeDtypeStruct((16, FT), BF16),
            jax.ShapeDtypeStruct((16, FT), BF16),
            jax.ShapeDtypeStruct((4, 4, 16, FT), BF16),
            jax.ShapeDtypeStruct((4, 4, 16, FT), BF16),
            jax.ShapeDtypeStruct((ITEMS, 2, 4, 2, 32, NU), BF16),
        ),
        in_specs=[vmem, vmem, smem, smem, hbm, hbm],
        out_specs=(vmem, vmem, hbm, hbm, hbm),
        scratch_shapes=[
            pltpu.VMEM((CAP + 1, BLK, BLK), BF16),
            pltpu.VMEM((CAP + 1, BLK, BLK), BF16),
            pltpu.VMEM((FT, UT), BF16),
            pltpu.VMEM((UT, FT), BF16),
            pltpu.VMEM((4, 4, 16, FT), BF16),
            pltpu.VMEM((4, 4, 16, FT), BF16),
            pltpu.VMEM((ITEMS, 2, 4, 2, 32, NU), BF16),
            pltpu.VMEM((ITEMS, 4, 2, 32, NU), BF16),
            pltpu.VMEM((ITEMS, 2, 32, NU), BF16),
            pltpu.VMEM((ITEMS, 2, 32, NU), BF16),
            pltpu.VMEM((ITEMS, 32, NU), BF16),
            pltpu.VMEM((ITEMS, 32, NU), BF16),
            pltpu.VMEM((ITEMS, 2, 4, 2, 32, NU), BF16),
            pltpu.VMEM((TOK, FT), F32),
            pltpu.VMEM((TOK, FT), F32),
            pltpu.VMEM((4, 4, 16, FT), BF16),
            pltpu.VMEM((4, 4, 16, FT), BF16),
            pltpu.VMEM((6, 2, 16, FT), BF16),
            pltpu.VMEM((6, 2, 16, FT), BF16),
            pltpu.VMEM((6, 16, FT // 2), BF16),
            pltpu.VMEM((6, 16, FT // 2), BF16),
            pltpu.SemaphoreType.DMA((N_SEMS,)),
            pltpu.SemaphoreType.DMA((N_SEMS,)),
            pltpu.SemaphoreType.DMA((5,)),
        ],
        compiler_params=pltpu.CompilerParams(
            collective_id=0, has_side_effects=True, vmem_limit_bytes=60 * 1024 * 1024
        ),
        cost_estimate=pl.CostEstimate(flops=flops, bytes_accessed=17_000_000, transcendentals=200_000),
        name="ffn_fused",
    )(tokens, out_grad, inv1, inv2, w1, w2)


STEP = 18


def wgrad_kernel(idx1_ref, idx2_ref, tok_ref, g_ref, ag_ref, gw1_ref, gw2_ref, tok_t, g_b, act_t, pre_b):
    step = pl.program_id(0)

    @pl.when(step == 0)
    def _():
        def feats(i, carry):
            here = pl.ds(pl.multiple_of(i * BLK, BLK), BLK)
            tok_t[i] = tok_ref[:, :, :, here].reshape(TOK, BLK).T
            g_b[i] = g_ref[:, :, :, here].reshape(TOK, BLK)
            return carry

        lax.fori_loop(0, FB, feats, 0)
        per = NU // BLK

        def units(j, carry):
            u, n = j // per, j % per
            here = pl.ds(pl.multiple_of(n * BLK, BLK), BLK)
            act_t[j] = ag_ref[u, :, :, 0, :, here].reshape(TOK, BLK).T
            pre_b[j] = ag_ref[u, :, :, 1, :, here].reshape(TOK, BLK)
            return carry

        lax.fori_loop(0, UB, units, 0)

    def slot(n, carry):
        s = step * STEP + n
        i, j = idx1_ref[2 * s], idx1_ref[2 * s + 1]
        jj = jnp.minimum(j, UB - 1)
        value = jnp.dot(tok_t[i], pre_b[jj], preferred_element_type=F32)
        gw1_ref[n] = jnp.where(j < UB, value, 0.0).astype(BF16)
        i, j = idx2_ref[2 * s], idx2_ref[2 * s + 1]
        jj = jnp.minimum(j, FB - 1)
        value = jnp.dot(act_t[i], g_b[jj], preferred_element_type=F32)
        gw2_ref[n] = jnp.where(j < FB, value, 0.0).astype(BF16)
        return carry

    lax.fori_loop(0, STEP, slot, 0, unroll=6)


def wgrad(idx1, idx2, tok_all, g_all, ag):
    smem = pl.BlockSpec(memory_space=pltpu.SMEM)
    vmem = pl.BlockSpec(memory_space=pltpu.VMEM)
    out = pl.BlockSpec((STEP, BLK, BLK), lambda s: (s, 0, 0))
    shape = jax.ShapeDtypeStruct((CAP, BLK, BLK), BF16)
    return pl.pallas_call(
        wgrad_kernel,
        grid=(CAP // STEP,),
        out_shape=(shape, shape),
        in_specs=[smem, smem, vmem, vmem, vmem],
        out_specs=(out, out),
        scratch_shapes=[
            pltpu.VMEM((FB, BLK, TOK), BF16),
            pltpu.VMEM((FB, TOK, BLK), BF16),
            pltpu.VMEM((UB, BLK, TOK), BF16),
            pltpu.VMEM((UB, TOK, BLK), BF16),
        ],
        compiler_params=pltpu.CompilerParams(vmem_limit_bytes=48 * 1024 * 1024),
        cost_estimate=pl.CostEstimate(
            flops=2 * 2 * CAP * BLK * BLK * TOK, bytes_accessed=16_500_000, transcendentals=0
        ),
        name="ffn_wgrad",
    )(idx1, idx2, tok_all, g_all, ag)


def inverse(rows, cols, width, count):
    target = jnp.where(cols < width, rows * width + cols, count)
    places = jnp.arange(count, dtype=jnp.int32)
    slots = jnp.arange(CAP, dtype=jnp.int32)
    hit = target[None, :] == places[:, None]
    return jnp.min(jnp.where(hit, slots[None, :], CAP), axis=1).astype(jnp.int32)


def body(tokens, out_grad, w1_blocks, w1_index, w2_blocks, w2_index):
    inv1 = inverse(w1_index[:, 0], w1_index[:, 1], UB, FB * UB)
    inv2 = inverse(w2_index[:, 0], w2_index[:, 1], FB, FB * UB)
    output, grad_input, tok_all, g_all, ag = fused(tokens, out_grad, inv1, inv2, w1_blocks, w2_blocks)
    grad_one, grad_two = wgrad(w1_index.reshape(-1), w2_index.reshape(-1), tok_all, g_all, ag)
    return output, grad_input, grad_one, grad_two


def solution(mesh):
    return jax.shard_map(
        body,
        mesh=mesh,
        in_specs=(
            P("row", "col"),
            P("row", "col"),
            P(("row", "col"), None, None),
            P(("row", "col"), None),
            P(("row", "col"), None, None),
            P(("row", "col"), None),
        ),
        out_specs=(
            P("row", "col"),
            P("row", "col"),
            P(("row", "col"), None, None),
            P(("row", "col"), None, None),
        ),
        check_vma=False,
    )
```

```python
import jax
import jax.numpy as jnp
from jax import lax
from jax.experimental import pallas as pl
from jax.experimental.pallas import tpu as pltpu
from jax.sharding import PartitionSpec as P

MESH = pl.DeviceIdType.MESH
BLK = 128
CAP = 180
FB = 12
UB = 24
FT = FB * BLK
UT = UB * BLK
TOK = 256
ITEMS = 4
NU = UT // ITEMS
UPI = UB // ITEMS
PER = UPI * FB
F32 = jnp.float32
BF16 = jnp.bfloat16
I32 = jnp.int32
NT = (((1,), (1,)), ((), ()))

ORDER = (
    "F0h F0g F1h 10h", "F1g 10g 11h F2h", "11g 20h F2g 12h", "20g F3h 21h 12g",
    "F3g 21g 13h 30h", "22h 30g 13g 31h", "22g 31g T0h 23h", "40h 50h 32h 40g",
    "50g 23g 51h 41h", "32g 51g 41g 33h", "52h 60h 60g 42h", "33g B0h 42g 61h",
    "B0g 43h 61g 52g", "53h B1h 43g 62h", "B1g 62g 63h 53g", "B2h 63g B2g B3h",
    "C0h B3g C0g W0h", "W0g C1h C1g W1h", "C2h C2g W1g C3h", "C3g W2h C4h C4g",
    "W2g W3h W3g C5h", "C5g",
)


def gelu_pair(value):
    cubic_term = 0.044715 * value * value * value
    tangent = jnp.tanh(0.7978845608 * (value + cubic_term))
    result = 0.5 * value * (1.0 + tangent)
    derivative = 0.5 * (1.0 + tangent) + 0.5 * value * (1.0 - tangent * tangent) * 0.7978845608 * (
        1.0 + 3.0 * 0.044715 * value * value
    )
    return (result, derivative)


def add(a, b):
    return (a.astype(F32) + b.astype(F32)).astype(BF16)


def fused_kernel(
    tok_ref,
    grad_ref,
    idx1_ref,
    idx2_ref,
    w1_hbm,
    w2_hbm,
    out_ref,
    gin_ref,
    dw1_hbm,
    dw2_hbm,
    w1v,
    w2v,
    dense1,
    dense2,
    full,
    part,
    rc,
    m1a,
    m1b,
    m2,
    slope,
    ag,
    acc,
    po,
    c1,
    c2,
    tok_t,
    act_t,
    inv_v,
    inv_s,
    send_sems,
    recv_sems,
    local_sems,
):
    row = lax.axis_index("row")
    col = lax.axis_index("col")
    y, z = row // 4, row % 4
    x, k = col // 2, col % 2
    yr, yl, yo = (y + 1) % 4, (y + 3) % 4, (y + 2) % 4
    zr, zl, zo = (z + 1) % 4, (z + 3) % 4, (z + 2) % 4
    xr, xl, xo = (x + 1) % 4, (x + 3) % 4, (x + 2) % 4
    sib = (row, x * 2 + 1 - k)
    dev_xr, dev_xl = (row, xr * 2 + k), (row, xl * 2 + k)
    dev_y = tuple((p * 4 + z, col) for p in (yr, yl, yo))
    dev_z = tuple((y * 4 + p, col) for p in (zr, zl, zo))

    load1 = pltpu.make_async_copy(w1_hbm, w1v.at[pl.ds(0, CAP)], local_sems.at[0])
    load2 = pltpu.make_async_copy(w2_hbm, w2v.at[pl.ds(0, CAP)], local_sems.at[1])
    load1.start()
    load2.start()

    barrier = pltpu.get_barrier_semaphore()
    for dev in (sib, dev_xr, dev_xl) + dev_y + dev_z:
        pl.semaphore_signal(barrier, inc=1, device_id=dev, device_id_type=MESH)

    full[0, y, z] = tok_ref[...]
    full[1, y, z] = grad_ref[...]
    w1v[CAP] = jnp.zeros((BLK, BLK), BF16)
    w2v[CAP] = jnp.zeros((BLK, BLK), BF16)
    inv_v[...] = jnp.full((8, BLK), CAP, I32)
    for n, (idx, width) in enumerate(((idx1_ref, UB), (idx2_ref, FB))):
        i, j = idx[0:1, :], idx[1:2, :]
        target = jnp.where(j < width, i * width + j, 511)
        spread = jnp.broadcast_to(target, (BLK, CAP)).T
        slots = lax.broadcasted_iota(I32, (CAP, BLK), 0)
        places = lax.broadcasted_iota(I32, (CAP, BLK), 1)
        for m in range(3):
            found = jnp.where(spread == places + m * BLK, slots, CAP)
            inv_v[n * 3 + m : n * 3 + m + 1, :] = jnp.min(found, axis=0, keepdims=True)
    table = pltpu.make_async_copy(inv_v, inv_s, local_sems.at[2])
    table.start()
    pl.semaphore_wait(barrier, 9)

    started = []

    def send(src, dst, dev):
        n = len(started)
        copy = pltpu.make_async_remote_copy(
            src_ref=src,
            dst_ref=dst,
            send_sem=send_sems.at[n],
            recv_sem=recv_sems.at[n],
            device_id=dev,
            device_id_type=MESH,
        )
        copy.start()
        started.append(copy)
        return copy

    def slot(a, p, q):
        return full.at[a, q, p] if a == 0 else full.at[a, p, q]

    near = ((z, zr, zl, zo), (y, yr, yl, yo))
    own = (y, z)
    first = (dev_z, dev_y)
    second = (dev_y, dev_z)

    def spread_to(ref, devs):
        return [send(ref, ref, dev) for dev in devs]

    stage_a = [spread_to(slot(a, near[a][0], own[a]), first[a]) for a in (0, 1)]
    stage_b = [[spread_to(slot(a, near[a][0], own[a]), second[a])] for a in (0, 1)]

    def fill1(i, carry):
        for j in range(UB):
            p = i * UB + j
            dense1[pl.ds(pl.multiple_of(i * BLK, BLK), BLK), pl.ds(j * BLK, BLK)] = w1v[inv_s[p >> 7, p & 127]]
        return carry

    def fill2(i, carry):
        for j in range(FB):
            p = i * FB + j
            dense2[pl.ds(pl.multiple_of(i * BLK, BLK), BLK), pl.ds(j * BLK, BLK)] = w2v[inv_s[3 + (p >> 7), p & 127]]
        return carry

    table.wait()
    load1.wait()
    lax.fori_loop(0, FB, fill1, 0)
    for step, mirror in ((1, 1), (2, 0), (3, 2)):
        for a in (0, 1):
            stage_a[a][mirror].wait_recv()
            stage_b[a].append(spread_to(slot(a, near[a][step], own[a]), second[a]))
        if step == 2:
            load2.wait()
            lax.fori_loop(0, UB, fill2, 0)
    for a in (0, 1):
        for copies in stage_b[a]:
            for copy in copies:
                copy.wait_recv()

    ahead = (dev_xr, dev_xl)
    behind = (dev_xl, dev_xr)
    x_ahead = (xr, xl)
    x_behind = (xl, xr)
    flight = {}

    def step_f(u, a):
        tokens = full[a].reshape(TOK, FT)
        if a == 0:
            hidden = jnp.dot(tokens, dense1[:, pl.ds(u * NU, NU)], preferred_element_type=F32)
        else:
            hidden = lax.dot_general(tokens, dense2[pl.ds(u * NU, NU), :], NT, preferred_element_type=F32)
        part[a, u] = hidden.astype(BF16).reshape(2, 4, 32, NU)
        flight["core", u, a] = send(part.at[a, u, 1 - k], rc.at[a, u], sib)

    def step_1(u, a):
        flight["core", u, a].wait_recv()
        for where in (xo, x_behind[a], x_ahead[a], x):
            part[a, u, k, where] = add(part[a, u, k, where], rc[a, u, where])
        flight["m1a", u, a] = send(part.at[a, u, k, xo], m1a.at[a, u], ahead[a])
        flight["m1b", u, a] = send(part.at[a, u, k, x_behind[a]], m1b.at[a, u], behind[a])

    def step_2(u, a):
        flight["m1a", u, a].wait_recv()
        part[a, u, k, x_ahead[a]] = add(part[a, u, k, x_ahead[a]], m1a[a, u])
        flight["m2", u, a] = send(part.at[a, u, k, x_ahead[a]], m2.at[a, u], ahead[a])

    def step_3(u, a):
        flight["m1b", u, a].wait_recv()
        flight["m2", u, a].wait_recv()
        total = part[a, u, k, x].astype(F32) + m1b[a, u].astype(F32) + m2[a, u].astype(F32)
        if a == 0:
            act, rate = gelu_pair(total)
            slope[u] = rate
            ag[a, u, k, x] = act.astype(BF16)
        else:
            ag[a, u, k, x] = (total * slope[u]).astype(BF16)
        mine = ag.at[a, u, k, x]
        flight["agd", u, a] = send(mine, mine, ahead[a])
        flight["ago", u, a] = send(mine, mine, behind[a])
        flight["s0", u, a] = send(mine, mine, sib)

    def step_4(u, a):
        flight["agd", u, a].wait_recv()
        got = ag.at[a, u, k, x_behind[a]]
        flight["fwd", u, a] = send(got, got, ahead[a])
        flight["s1", u, a] = send(got, got, sib)

    def step_5(u, a):
        flight["ago", u, a].wait_recv()
        got = ag.at[a, u, k, x_ahead[a]]
        flight["s2", u, a] = send(got, got, sib)

    def step_6(u, a):
        flight["fwd", u, a].wait_recv()
        got = ag.at[a, u, k, xo]
        flight["s3", u, a] = send(got, got, sib)

    def step_b(u, a):
        for name in ("s0", "s1", "s2", "s3"):
            flight[name, u, a].wait_recv()
        base = pl.ds(u * NU, NU)
        width = FT // 2
        for n in range(2):
            here = pl.ds(n * width, width)
            units = ag[a, u].reshape(TOK, NU)
            if a == 0:
                value = jnp.dot(units, dense2[base, here], preferred_element_type=F32)
            else:
                value = lax.dot_general(units, dense1[here, base], NT, preferred_element_type=F32)
            if u > 0:
                value = value + acc[a, :, here]
            if u < ITEMS - 1:
                acc[a, :, here] = value
            else:
                po[a, :, :, :, here] = value.astype(BF16).reshape(4, 4, 16, width)

    def step_t(u, a):
        for i in range(FB):
            tok_t[pl.ds(i * BLK, BLK), :] = full[0, :, :, :, pl.ds(i * BLK, BLK)].reshape(TOK, BLK).T

    saves = {}

    def step_w(u, a):
        stage, target = ((w2v, dw2_hbm), (w1v, dw1_hbm))[a]
        base = (u % 2) * PER
        if u >= 2:
            saves[u - 2, a].wait()
        if a == 1:
            for n in range(NU // 256):
                pre = ag[1, u, :, :, :, pl.ds(n * 256, 256)].reshape(TOK, 256)
                value = jnp.dot(tok_t[...], pre, preferred_element_type=F32).astype(BF16)
                for c in range(2):
                    piece = value[:, c * BLK : (c + 1) * BLK].reshape(FB, BLK, BLK)
                    stage[pl.ds(base + (2 * n + c) * FB, FB)] = piece
        else:
            for i in range(UPI):
                act_t[pl.ds(i * BLK, BLK), :] = ag[0, u, :, :, :, pl.ds(i * BLK, BLK)].reshape(TOK, BLK).T
            for n in range(FT // 256):
                grads = full[1, :, :, :, pl.ds(n * 256, 256)].reshape(TOK, 256)
                value = jnp.dot(act_t[...], grads, preferred_element_type=F32).astype(BF16)
                for c in range(2):
                    piece = value[:, c * BLK : (c + 1) * BLK].reshape(UPI, BLK, BLK)
                    stage[pl.ds(base + (2 * n + c) * UPI, UPI)] = piece
        save = pltpu.make_async_copy(
            stage.at[pl.ds(base, PER)], target.at[pl.ds(u * PER, PER)], local_sems.at[3 + 2 * u + a]
        )
        save.start()
        saves[u, a] = save

    def piece(a, p, q):
        return po.at[a, p, q] if a == 0 else po.at[a, q, p]

    far = ((zo, zr, zl, z), (yo, yr, yl, y))
    mine_p = (y, z)
    peers = ((yr, yl, yo), (zr, zl, zo))
    peer_devs = (dev_y, dev_z)
    last_devs = ((dev_z[2], dev_z[0], dev_z[1]), (dev_y[2], dev_y[0], dev_y[1]))

    def step_c(u, a):
        if u == 0:
            for n in range(4):
                flight["c1", n, a] = [
                    send(piece(a, peers[a][d], far[a][n]), c1.at[a, n, d], peer_devs[a][d]) for d in (2, 0, 1)
                ]
        elif u <= 4:
            n = u - 1
            for copy in flight["c1", n, a]:
                copy.wait_recv()
            spot = piece(a, mine_p[a], far[a][n])
            total = spot[...].astype(F32)
            for d in range(3):
                total = total + c1[a, n, d].astype(F32)
            spot[...] = total.astype(BF16)
            if n < 3:
                flight["c2", n, a] = send(spot, c2.at[a, n], last_devs[a][n])
        else:
            total = piece(a, mine_p[a], far[a][3])[...].astype(F32)
            for n in range(3):
                flight["c2", n, a].wait_recv()
                total = total + c2[a, n].astype(F32)
            (out_ref, gin_ref)[a][...] = total.astype(BF16)

    steps = {
        "F": step_f,
        "1": step_1,
        "2": step_2,
        "3": step_3,
        "4": step_4,
        "5": step_5,
        "6": step_6,
        "B": step_b,
        "T": step_t,
        "W": step_w,
        "C": step_c,
    }
    for line in ORDER:
        for name in line.split():
            steps[name[0]](int(name[1]), "hg".index(name[2]))

    for copy in started:
        copy.wait_send()
    for u in range(max(ITEMS - 2, 0), ITEMS):
        saves[u, 0].wait()
        saves[u, 1].wait()


N_SEMS = 30 + 22 * ITEMS + 30


def fused(tokens, out_grad, idx1, idx2, w1, w2):
    vmem = pl.BlockSpec(memory_space=pltpu.VMEM)
    hbm = pl.BlockSpec(memory_space=pl.ANY)
    flops = 6 * 2 * TOK * FT * UT
    return pl.pallas_call(
        fused_kernel,
        out_shape=(
            jax.ShapeDtypeStruct((16, FT), BF16),
            jax.ShapeDtypeStruct((16, FT), BF16),
            jax.ShapeDtypeStruct((FB * UB, BLK, BLK), BF16),
            jax.ShapeDtypeStruct((FB * UB, BLK, BLK), BF16),
        ),
        in_specs=[vmem, vmem, vmem, vmem, hbm, hbm],
        out_specs=(vmem, vmem, hbm, hbm),
        scratch_shapes=[
            pltpu.VMEM((CAP + 1, BLK, BLK), BF16),
            pltpu.VMEM((CAP + 1, BLK, BLK), BF16),
            pltpu.VMEM((FT, UT), BF16),
            pltpu.VMEM((UT, FT), BF16),
            pltpu.VMEM((2, 4, 4, 16, FT), BF16),
            pltpu.VMEM((2, ITEMS, 2, 4, 32, NU), BF16),
            pltpu.VMEM((2, ITEMS, 4, 32, NU), BF16),
            pltpu.VMEM((2, ITEMS, 32, NU), BF16),
            pltpu.VMEM((2, ITEMS, 32, NU), BF16),
            pltpu.VMEM((2, ITEMS, 32, NU), BF16),
            pltpu.VMEM((ITEMS, 32, NU), F32),
            pltpu.VMEM((2, ITEMS, 2, 4, 32, NU), BF16),
            pltpu.VMEM((2, TOK, FT), F32),
            pltpu.VMEM((2, 4, 4, 16, FT), BF16),
            pltpu.VMEM((2, 4, 3, 16, FT), BF16),
            pltpu.VMEM((2, 3, 16, FT), BF16),
            pltpu.VMEM((FT, TOK), BF16),
            pltpu.VMEM((NU, TOK), BF16),
            pltpu.VMEM((8, BLK), I32),
            pltpu.SMEM((8, BLK), I32),
            pltpu.SemaphoreType.DMA((N_SEMS,)),
            pltpu.SemaphoreType.DMA((N_SEMS,)),
            pltpu.SemaphoreType.DMA((3 + 2 * ITEMS,)),
        ],
        compiler_params=pltpu.CompilerParams(
            collective_id=0, has_side_effects=True, vmem_limit_bytes=60 * 1024 * 1024
        ),
        cost_estimate=pl.CostEstimate(flops=flops, bytes_accessed=31_000_000, transcendentals=200_000),
        name="ffn_fused",
    )(tokens, out_grad, idx1, idx2, w1, w2)


def place_kernel(
    idx1_ref, idx2_ref, dw1, dw2, out_in, gin_in, gw1, gw2, out, gin, zero, sem1, sem2, sem3
):
    zero[...] = jnp.zeros((BLK, BLK), BF16)
    outs = (pltpu.make_async_copy(out_in, out, sem3.at[0]), pltpu.make_async_copy(gin_in, gin, sem3.at[1]))
    for copy in outs:
        copy.start()

    def one(s, carry):
        i, j = idx1_ref[0, s], idx1_ref[1, s]
        kept = j < UB

        @pl.when(kept)
        def _():
            pltpu.make_async_copy(dw1.at[j * FB + i], gw1.at[s], sem1).start()

        @pl.when(jnp.logical_not(kept))
        def _():
            pltpu.make_async_copy(zero, gw1.at[s], sem1).start()

        i2, j2 = idx2_ref[0, s], idx2_ref[1, s]
        kept2 = j2 < FB

        @pl.when(kept2)
        def _():
            pltpu.make_async_copy(dw2.at[(i2 // UPI) * PER + j2 * UPI + i2 % UPI], gw2.at[s], sem2).start()

        @pl.when(jnp.logical_not(kept2))
        def _():
            pltpu.make_async_copy(zero, gw2.at[s], sem2).start()

        return carry

    lax.fori_loop(0, CAP, one, 0, unroll=4)
    pltpu.make_async_copy(dw1.at[pl.ds(0, CAP)], gw1, sem1).wait()
    pltpu.make_async_copy(dw2.at[pl.ds(0, CAP)], gw2, sem2).wait()
    for copy in outs:
        copy.wait()


def place(idx1, idx2, dw1, dw2, out, gin):
    smem = pl.BlockSpec(memory_space=pltpu.SMEM)
    hbm = pl.BlockSpec(memory_space=pl.ANY)
    shape = jax.ShapeDtypeStruct((CAP, BLK, BLK), BF16)
    small = jax.ShapeDtypeStruct((16, FT), BF16)
    return pl.pallas_call(
        place_kernel,
        out_shape=(shape, shape, small, small),
        in_specs=[smem, smem, hbm, hbm, hbm, hbm],
        out_specs=(hbm, hbm, hbm, hbm),
        scratch_shapes=[
            pltpu.VMEM((BLK, BLK), BF16),
            pltpu.SemaphoreType.DMA,
            pltpu.SemaphoreType.DMA,
            pltpu.SemaphoreType.DMA((2,)),
        ],
        cost_estimate=pl.CostEstimate(flops=0, bytes_accessed=24_000_000, transcendentals=0),
        name="ffn_place",
    )(idx1, idx2, dw1, dw2, out, gin)


def body(tokens, out_grad, w1_blocks, w1_index, w2_blocks, w2_index):
    idx1, idx2 = w1_index.T, w2_index.T
    output, grad_input, dw1, dw2 = fused(tokens, out_grad, idx1, idx2, w1_blocks, w2_blocks)
    grad_one, grad_two, output, grad_input = place(idx1, idx2, dw1, dw2, output, grad_input)
    return output, grad_input, grad_one, grad_two


def solution(mesh):
    return jax.shard_map(
        body,
        mesh=mesh,
        in_specs=(
            P("row", "col"),
            P("row", "col"),
            P(("row", "col"), None, None),
            P(("row", "col"), None),
            P(("row", "col"), None, None),
            P(("row", "col"), None),
        ),
        out_specs=(
            P("row", "col"),
            P("row", "col"),
            P(("row", "col"), None, None),
            P(("row", "col"), None, None),
        ),
        check_vma=False,
    )
```

```python
import jax
import jax.numpy as jnp
from jax import lax
from jax.experimental import pallas as pl
from jax.experimental.pallas import tpu as pltpu
from jax.sharding import PartitionSpec as P

MESH = pl.DeviceIdType.MESH
BLK = 128
CAP = 180
FB = 12
UB = 24
FT = FB * BLK
UT = UB * BLK
TOK = 256
ITEMS = 4
NU = UT // ITEMS
UPI = UB // ITEMS
PER = UPI * FB
F32 = jnp.float32
BF16 = jnp.bfloat16
I32 = jnp.int32
NONE = FB * UB
NT = (((1,), (1,)), ((), ()))

ORDER = (
    "F0h F0g F1h 10h", "F1g 10g 11h F2h", "11g 20h F2g 12h", "20g F3h 21h 12g",
    "F3g 21g 13h 30h", "22h 30g 13g 31h", "22g 31g T0h 23h", "40h 50h 32h 40g",
    "50g 23g 51h 41h", "32g 51g 41g 33h", "52h 60h 60g 42h", "33g B0h 42g 61h",
    "B0g 43h 61g 52g", "53h B1h 43g 62h", "B1g 62g 63h 53g", "B2h 63g B2g B3h",
    "C0h B3g C0g W0g", "W1g C1h C1g W2g", "C2h C2g W3g C3h", "C3g S0g C4h C4g",
    "W0h W1h C5h C5g", "W2h W3h S0h",
)


def gelu_pair(value):
    cubic_term = 0.044715 * value * value * value
    tangent = jnp.tanh(0.7978845608 * (value + cubic_term))
    result = 0.5 * value * (1.0 + tangent)
    derivative = 0.5 * (1.0 + tangent) + 0.5 * value * (1.0 - tangent * tangent) * 0.7978845608 * (
        1.0 + 3.0 * 0.044715 * value * value
    )
    return (result, derivative)


def add(a, b):
    return (a.astype(F32) + b.astype(F32)).astype(BF16)


def fused_kernel(
    tok_hbm,
    grad_hbm,
    idx1_hbm,
    idx2_hbm,
    w1_hbm,
    w2_hbm,
    out_ref,
    gin_ref,
    dw1_hbm,
    dw2_hbm,
    wv,
    dense1,
    dense2,
    full,
    part,
    m1a,
    m1b,
    m2,
    slope,
    ag,
    acc,
    po,
    c1,
    c2,
    tok_t,
    act_t,
    idx_v,
    pos_v,
    pos_s,
    inv_v,
    inv_s,
    send_sems,
    recv_sems,
    local_sems,
):
    row = lax.axis_index("row")
    col = lax.axis_index("col")
    y, z = row // 4, row % 4
    x, k = col // 2, col % 2
    yr, yl, yo = (y + 1) % 4, (y + 3) % 4, (y + 2) % 4
    zr, zl, zo = (z + 1) % 4, (z + 3) % 4, (z + 2) % 4
    xr, xl, xo = (x + 1) % 4, (x + 3) % 4, (x + 2) % 4
    sib = (row, x * 2 + 1 - k)
    dev_xr, dev_xl = (row, xr * 2 + k), (row, xl * 2 + k)
    dev_y = tuple((p * 4 + z, col) for p in (yr, yl, yo))
    dev_z = tuple((y * 4 + p, col) for p in (zr, zl, zo))

    load1 = pltpu.make_async_copy(w1_hbm, wv.at[pl.ds(0, CAP)], local_sems.at[0])
    load2 = pltpu.make_async_copy(w2_hbm, wv.at[pl.ds(0, CAP)], local_sems.at[1])
    loads = [
        pltpu.make_async_copy(source, target, local_sems.at[3 + n])
        for n, (source, target) in enumerate(
            (
                (idx1_hbm, idx_v.at[0]),
                (idx2_hbm, idx_v.at[1]),
                (tok_hbm, full.at[0, y, z]),
                (grad_hbm, full.at[1, y, z]),
            )
        )
    ]
    for load in loads:
        load.start()
    load1.start()

    barrier = pltpu.get_barrier_semaphore()
    for dev in (sib, dev_xr, dev_xl) + dev_y + dev_z:
        pl.semaphore_signal(barrier, inc=1, device_id=dev, device_id_type=MESH)

    for ref, last in ((wv, CAP), (dense1, NONE), (dense2, NONE)):
        ref[last] = jnp.zeros((BLK, BLK), BF16)
    loads[0].wait()
    loads[1].wait()
    inv_v[...] = jnp.full((8, BLK), CAP, I32)
    for n, (height, width) in enumerate(((FB, UB), (UB, FB))):
        i, j = idx_v[n, 0:1, :], idx_v[n, 1:2, :]
        target = jnp.where(j < width, j * height + i, NONE)
        pos_v[n : n + 1, :] = target
        spread = jnp.broadcast_to(target, (BLK, CAP)).T
        slots = lax.broadcasted_iota(I32, (CAP, BLK), 0)
        places = lax.broadcasted_iota(I32, (CAP, BLK), 1)
        for m in range(3):
            found = jnp.where(spread == places + m * BLK, slots, CAP)
            inv_v[n * 3 + m : n * 3 + m + 1, :] = jnp.min(found, axis=0, keepdims=True)
    table = pltpu.make_async_copy(inv_v, inv_s, local_sems.at[2])
    table.start()
    places_of = pltpu.make_async_copy(pos_v, pos_s, local_sems.at[7])
    places_of.start()
    for load in loads[2:]:
        load.wait()
    pl.semaphore_wait(barrier, 9)

    started = []

    def send(src, dst, dev):
        n = len(started)
        copy = pltpu.make_async_remote_copy(
            src_ref=src,
            dst_ref=dst,
            send_sem=send_sems.at[n],
            recv_sem=recv_sems.at[n],
            device_id=dev,
            device_id_type=MESH,
        )
        copy.start()
        started.append(copy)
        return copy

    def slot(a, p, q):
        return full.at[a, q, p] if a == 0 else full.at[a, p, q]

    near = ((z, zr, zl, zo), (y, yr, yl, yo))
    own = (y, z)
    first = (dev_z, dev_y)
    second = (dev_y, dev_z)

    def spread_to(ref, devs):
        return [send(ref, ref, dev) for dev in devs]

    stage_a = [spread_to(slot(a, near[a][0], own[a]), first[a]) for a in (0, 1)]
    stage_b = [[spread_to(slot(a, near[a][0], own[a]), second[a])] for a in (0, 1)]

    def fill(dense, first_row):
        def some(m, carry):
            for n in range(12):
                p = m * 12 + n
                dense[p] = wv[inv_s[first_row + (p >> 7), p & 127]]
            return carry

        lax.fori_loop(0, FB * UB // 12, some, 0)

    table.wait()
    places_of.wait()
    load1.wait()
    fill(dense1, 0)
    load2.start()
    for step, mirror in ((1, 1), (2, 0), (3, 2)):
        for a in (0, 1):
            stage_a[a][mirror].wait_recv()
            stage_b[a].append(spread_to(slot(a, near[a][step], own[a]), second[a]))
        if step == 2:
            load2.wait()
            fill(dense2, 3)
    for a in (0, 1):
        for copies in stage_b[a]:
            for copy in copies:
                copy.wait_recv()

    ahead = (dev_xr, dev_xl)
    behind = (dev_xl, dev_xr)
    x_ahead = (xr, xl)
    x_behind = (xl, xr)
    flight = {}

    def tile1(u, rows, count):
        return jnp.concatenate(
            [dense1[pl.ds(j * FB + rows, count)].reshape(count * BLK, BLK) for j in range(u * UPI, (u + 1) * UPI)], axis=1
        )

    def tile2(u, columns, count):
        return jnp.concatenate(
            [dense2[pl.ds(j * UB + u * UPI, UPI)].reshape(NU, BLK) for j in range(columns, columns + count)], axis=1
        )

    def step_f(u, a):
        tokens = full[a].reshape(TOK, FT)
        if a == 0:
            hidden = jnp.dot(tokens, tile1(u, 0, FB), preferred_element_type=F32)
        else:
            hidden = lax.dot_general(tokens, tile2(u, 0, FB), NT, preferred_element_type=F32)
        part[a, u] = hidden.astype(BF16).reshape(2, 4, 32, NU)
        flight["core", u, a] = send(part.at[a, u, 1 - k], ag.at[a, u, 1 - k], sib)

    def step_1(u, a):
        flight["core", u, a].wait_recv()
        for where in (xo, x_behind[a], x_ahead[a], x):
            part[a, u, k, where] = add(part[a, u, k, where], ag[a, u, k, where])
        flight["m1a", u, a] = send(part.at[a, u, k, xo], m1a.at[a, u], ahead[a])
        flight["m1b", u, a] = send(part.at[a, u, k, x_behind[a]], m1b.at[a, u], behind[a])

    def step_2(u, a):
        flight["m1a", u, a].wait_recv()
        part[a, u, k, x_ahead[a]] = add(part[a, u, k, x_ahead[a]], m1a[a, u])
        flight["m2", u, a] = send(part.at[a, u, k, x_ahead[a]], m2.at[a, u], ahead[a])

    def step_3(u, a):
        flight["m1b", u, a].wait_recv()
        flight["m2", u, a].wait_recv()
        total = part[a, u, k, x].astype(F32) + m1b[a, u].astype(F32) + m2[a, u].astype(F32)
        if a == 0:
            act, rate = gelu_pair(total)
            slope[u] = rate
            ag[a, u, k, x] = act.astype(BF16)
        else:
            ag[a, u, k, x] = (total * slope[u]).astype(BF16)
        mine = ag.at[a, u, k, x]
        flight["agd", u, a] = send(mine, mine, ahead[a])
        flight["ago", u, a] = send(mine, mine, behind[a])
        flight["s0", u, a] = send(mine, mine, sib)

    def step_4(u, a):
        flight["agd", u, a].wait_recv()
        got = ag.at[a, u, k, x_behind[a]]
        flight["fwd", u, a] = send(got, got, ahead[a])
        flight["s1", u, a] = send(got, got, sib)

    def step_5(u, a):
        flight["ago", u, a].wait_recv()
        got = ag.at[a, u, k, x_ahead[a]]
        flight["s2", u, a] = send(got, got, sib)

    def step_6(u, a):
        flight["fwd", u, a].wait_recv()
        got = ag.at[a, u, k, xo]
        flight["s3", u, a] = send(got, got, sib)

    def step_b(u, a):
        for name in ("s0", "s1", "s2", "s3"):
            flight[name, u, a].wait_recv()
        width = FT // 2
        half = FB // 2
        for n in range(2):
            here = pl.ds(n * width, width)
            units = ag[a, u].reshape(TOK, NU)
            if a == 0:
                value = jnp.dot(units, tile2(u, n * half, half), preferred_element_type=F32)
            else:
                value = lax.dot_general(units, tile1(u, n * half, half), NT, preferred_element_type=F32)
            if u > 0:
                value = value + acc[a, :, here]
            if u < ITEMS - 1:
                acc[a, :, here] = value
            else:
                po[a, :, :, :, here] = value.astype(BF16).reshape(4, 4, 16, width)

    def step_t(u, a):
        for i in range(FB):
            tok_t[pl.ds(i * BLK, BLK), :] = full[0, :, :, :, pl.ds(i * BLK, BLK)].reshape(TOK, BLK).T

    def step_w(u, a):
        if a == 1:
            pre = ag[1, u].reshape(TOK, NU)
            value = jnp.dot(tok_t[...], pre, preferred_element_type=F32).astype(BF16)
            for c in range(UPI):
                dense1[pl.ds((u * UPI + c) * FB, FB)] = value[:, c * BLK : (c + 1) * BLK].reshape(FB, BLK, BLK)
        else:
            for i in range(UPI):
                act_t[pl.ds(i * BLK, BLK), :] = ag[0, u, :, :, :, pl.ds(i * BLK, BLK)].reshape(TOK, BLK).T
            grads = full[1].reshape(TOK, FT)
            value = jnp.dot(act_t[...], grads, preferred_element_type=F32).astype(BF16)
            for c in range(FB):
                dense2[pl.ds(c * UB + u * UPI, UPI)] = value[:, c * BLK : (c + 1) * BLK].reshape(UPI, BLK, BLK)

    saves = []

    def step_s(u, a):
        dense, target = ((dense2, dw2_hbm), (dense1, dw1_hbm))[a]
        for save in saves:
            save.wait()

        def some(m, carry):
            for n in range(12):
                wv[m * 12 + n] = dense[pos_s[1 - a, m * 12 + n]]
            return carry

        lax.fori_loop(0, CAP // 12, some, 0)
        save = pltpu.make_async_copy(wv.at[pl.ds(0, CAP)], target, local_sems.at[9 + a])
        save.start()
        saves.append(save)

    def piece(a, p, q):
        return po.at[a, p, q] if a == 0 else po.at[a, q, p]

    far = ((zo, zr, zl, z), (yo, yr, yl, y))
    mine_p = (y, z)
    peers = ((yr, yl, yo), (zr, zl, zo))
    peer_devs = (dev_y, dev_z)
    last_devs = ((dev_z[2], dev_z[0], dev_z[1]), (dev_y[2], dev_y[0], dev_y[1]))

    def step_c(u, a):
        if u == 0:
            for n in range(4):
                flight["c1", n, a] = [
                    send(piece(a, peers[a][d], far[a][n]), c1.at[a, n, d], peer_devs[a][d]) for d in (2, 0, 1)
                ]
        elif u <= 4:
            n = u - 1
            for copy in flight["c1", n, a]:
                copy.wait_recv()
            spot = piece(a, mine_p[a], far[a][n])
            total = spot[...].astype(F32)
            for d in range(3):
                total = total + c1[a, n, d].astype(F32)
            spot[...] = total.astype(BF16)
            if n < 3:
                flight["c2", n, a] = send(spot, c2.at[a, n], last_devs[a][n])
        else:
            total = piece(a, mine_p[a], far[a][3])[...].astype(F32)
            for n in range(3):
                flight["c2", n, a].wait_recv()
                total = total + c2[a, n].astype(F32)
            (out_ref, gin_ref)[a][...] = total.astype(BF16)

    steps = {
        "F": step_f,
        "1": step_1,
        "2": step_2,
        "3": step_3,
        "4": step_4,
        "5": step_5,
        "6": step_6,
        "B": step_b,
        "T": step_t,
        "W": step_w,
        "S": step_s,
        "C": step_c,
    }
    for line in ORDER:
        for name in line.split():
            steps[name[0]](int(name[1]), "hg".index(name[2]))

    for copy in started:
        copy.wait_send()
    saves[-1].wait()


N_SEMS = 30 + 22 * ITEMS + 30


def fused(tokens, out_grad, idx1, idx2, w1, w2):
    vmem = pl.BlockSpec(memory_space=pltpu.VMEM)
    hbm = pl.BlockSpec(memory_space=pl.ANY)
    flops = 6 * 2 * TOK * FT * UT
    return pl.pallas_call(
        fused_kernel,
        out_shape=(
            jax.ShapeDtypeStruct((16, FT), BF16),
            jax.ShapeDtypeStruct((16, FT), BF16),
            jax.ShapeDtypeStruct((CAP, BLK, BLK), BF16),
            jax.ShapeDtypeStruct((CAP, BLK, BLK), BF16),
        ),
        in_specs=[pl.BlockSpec(memory_space=pltpu.HBM)] * 6,
        out_specs=(vmem, vmem, hbm, hbm),
        scratch_shapes=[
            pltpu.VMEM((CAP + 1, BLK, BLK), BF16),
            pltpu.VMEM((NONE + 1, BLK, BLK), BF16),
            pltpu.VMEM((NONE + 1, BLK, BLK), BF16),
            pltpu.VMEM((2, 4, 4, 16, FT), BF16),
            pltpu.VMEM((2, ITEMS, 2, 4, 32, NU), BF16),
            pltpu.VMEM((2, ITEMS, 32, NU), BF16),
            pltpu.VMEM((2, ITEMS, 32, NU), BF16),
            pltpu.VMEM((2, ITEMS, 32, NU), BF16),
            pltpu.VMEM((ITEMS, 32, NU), F32),
            pltpu.VMEM((2, ITEMS, 2, 4, 32, NU), BF16),
            pltpu.VMEM((2, TOK, FT), F32),
            pltpu.VMEM((2, 4, 4, 16, FT), BF16),
            pltpu.VMEM((2, 4, 3, 16, FT), BF16),
            pltpu.VMEM((2, 3, 16, FT), BF16),
            pltpu.VMEM((FT, TOK), BF16),
            pltpu.VMEM((NU, TOK), BF16),
            pltpu.VMEM((2, 2, CAP), I32),
            pltpu.VMEM((2, CAP), I32),
            pltpu.SMEM((2, CAP), I32),
            pltpu.VMEM((8, BLK), I32),
            pltpu.SMEM((8, BLK), I32),
            pltpu.SemaphoreType.DMA((N_SEMS,)),
            pltpu.SemaphoreType.DMA((N_SEMS,)),
            pltpu.SemaphoreType.DMA((11,)),
        ],
        compiler_params=pltpu.CompilerParams(
            collective_id=0, has_side_effects=True, vmem_limit_bytes=42 * 1024 * 1024
        ),
        cost_estimate=pl.CostEstimate(flops=flops, bytes_accessed=31_000_000, transcendentals=200_000),
        name="ffn_fused",
    )(tokens, out_grad, idx1, idx2, w1, w2)


def place_kernel(dw1, dw2, out_in, gin_in, gw1, gw2, out, gin, sems):
    copies = [
        pltpu.make_async_copy(source, target, sems.at[n])
        for n, (source, target) in enumerate(((dw1, gw1), (dw2, gw2), (out_in, out), (gin_in, gin)))
    ]
    for copy in copies:
        copy.start()
    for copy in copies:
        copy.wait()


def place(dw1, dw2, out, gin):
    hbm = pl.BlockSpec(memory_space=pl.ANY)
    shape = jax.ShapeDtypeStruct((CAP, BLK, BLK), BF16)
    small = jax.ShapeDtypeStruct((16, FT), BF16)
    return pl.pallas_call(
        place_kernel,
        out_shape=(shape, shape, small, small),
        in_specs=[hbm, hbm, hbm, hbm],
        out_specs=(hbm, hbm, hbm, hbm),
        scratch_shapes=[pltpu.SemaphoreType.DMA((4,))],
        compiler_params=pltpu.CompilerParams(vmem_limit_bytes=2 * 1024 * 1024),
        cost_estimate=pl.CostEstimate(flops=0, bytes_accessed=24_000_000, transcendentals=0),
        name="ffn_place",
    )(dw1, dw2, out, gin)


def body(tokens, out_grad, w1_blocks, w1_index, w2_blocks, w2_index):
    idx1, idx2 = w1_index.T, w2_index.T
    tokens, out_grad, idx1, idx2 = [
        pltpu.with_memory_space_constraint(value, pltpu.HBM) for value in (tokens, out_grad, idx1, idx2)
    ]
    output, grad_input, dw1, dw2 = fused(tokens, out_grad, idx1, idx2, w1_blocks, w2_blocks)
    grad_one, grad_two, output, grad_input = place(dw1, dw2, output, grad_input)
    return output, grad_input, grad_one, grad_two


def solution(mesh):
    return jax.shard_map(
        body,
        mesh=mesh,
        in_specs=(
            P("row", "col"),
            P("row", "col"),
            P(("row", "col"), None, None),
            P(("row", "col"), None),
            P(("row", "col"), None, None),
            P(("row", "col"), None),
        ),
        out_specs=(
            P("row", "col"),
            P("row", "col"),
            P(("row", "col"), None, None),
            P(("row", "col"), None, None),
        ),
        check_vma=False,
    )
```

```python
import jax
import jax.numpy as jnp
from jax import lax
from jax.experimental import pallas as pl
from jax.experimental.pallas import tpu as pltpu
from jax.sharding import PartitionSpec as P

MESH = pl.DeviceIdType.MESH
BLK = 128
CAP = 180
FB = 12
UB = 24
FT = FB * BLK
UT = UB * BLK
TOK = 256
ITEMS = 6
NU = UT // ITEMS
UPI = UB // ITEMS
PER = UPI * FB
F32 = jnp.float32
BF16 = jnp.bfloat16
I32 = jnp.int32
NONE = FB * UB
NT = (((1,), (1,)), ((), ()))

ORDER = (
    "F0h F1h F2h F3h", "10h 11h F4h 12h", "F5h 13h F0g 14h", "F1g 20h 15h 21h",
    "F2g 10g 22h F3g", "11g 23h F4g 12g", "24h 30h 13g 25h", "T0h 31h 14g 20g",
    "32h 21g 33h 22g", "F5g 50h 34h 40h", "15g 23g 35h 51h", "41h 24g 42h 30g",
    "31g 52h 53h 43h", "44h 32g 60h 54h", "25g B0h 45h 33g", "55h 61h W0h 62h",
    "34g B1h 40g 50g", "B2h 41g 51g 64h", "63h W1h 52g 42g", "W2h B3h 65h 35g",
    "43g 53g B4h 44g", "54g B5h 60g 61g", "C0h 62g 45g 55g", "B0g 63g 64g B1g",
    "B2g B3g B4g C1h", "65g W3h C2h W4h", "B5g C0g C3h C4h", "W5h S0h W0g W1g",
    "W2g C1g W3g W4g", "C2g W5g S0g C3g", "C4g C5h C5g",
)


def gelu_pair(value):
    cubic_term = 0.044715 * value * value * value
    tangent = jnp.tanh(0.7978845608 * (value + cubic_term))
    result = 0.5 * value * (1.0 + tangent)
    derivative = 0.5 * (1.0 + tangent) + 0.5 * value * (1.0 - tangent * tangent) * 0.7978845608 * (
        1.0 + 3.0 * 0.044715 * value * value
    )
    return (result, derivative)


def add(a, b):
    return (a.astype(F32) + b.astype(F32)).astype(BF16)


def fused_kernel(
    tok_hbm,
    grad_hbm,
    idx1_hbm,
    idx2_hbm,
    w1_hbm,
    w2_hbm,
    out_ref,
    gin_ref,
    dw1_hbm,
    dw2_hbm,
    wv,
    dense1,
    dense2,
    full,
    part,
    m1a,
    mm,
    slope,
    ag,
    acc,
    po,
    c1,
    c2,
    tok_t,
    act_t,
    idx_v,
    pos_v,
    pos_s,
    inv_v,
    inv_s,
    send_sems,
    recv_sems,
    local_sems,
):
    row = lax.axis_index("row")
    col = lax.axis_index("col")
    y, z = row // 4, row % 4
    x, k = col // 2, col % 2
    yr, yl, yo = (y + 1) % 4, (y + 3) % 4, (y + 2) % 4
    zr, zl, zo = (z + 1) % 4, (z + 3) % 4, (z + 2) % 4
    xr, xl, xo = (x + 1) % 4, (x + 3) % 4, (x + 2) % 4
    sib = (row, x * 2 + 1 - k)
    dev_xr, dev_xl = (row, xr * 2 + k), (row, xl * 2 + k)
    dev_y = tuple((p * 4 + z, col) for p in (yr, yl, yo))
    dev_z = tuple((y * 4 + p, col) for p in (zr, zl, zo))

    load1 = pltpu.make_async_copy(w1_hbm, wv.at[pl.ds(0, CAP)], local_sems.at[0])
    load2 = pltpu.make_async_copy(w2_hbm, wv.at[pl.ds(0, CAP)], local_sems.at[1])
    loads = [
        pltpu.make_async_copy(source, target, local_sems.at[3 + n])
        for n, (source, target) in enumerate(
            (
                (idx1_hbm, idx_v.at[0]),
                (idx2_hbm, idx_v.at[1]),
                (tok_hbm, full.at[y * 4 + z]),
                (grad_hbm, full.at[16 + y * 4 + z]),
            )
        )
    ]
    for load in loads:
        load.start()
    load1.start()

    barrier = pltpu.get_barrier_semaphore()
    for dev in (sib, dev_xr, dev_xl) + dev_y + dev_z:
        pl.semaphore_signal(barrier, inc=1, device_id=dev, device_id_type=MESH)

    for load in loads[2:]:
        load.wait()
    pl.semaphore_wait(barrier, 9)

    used = [0]

    def fresh():
        used[0] += 1
        return used[0] - 1

    def send(src, dst, dev, group, recv=None):
        copy = pltpu.make_async_remote_copy(
            src_ref=src,
            dst_ref=dst,
            send_sem=send_sems.at[group],
            recv_sem=recv_sems.at[fresh() if recv is None else recv],
            device_id=dev,
            device_id_type=MESH,
        )
        copy.start()
        return copy

    def wait_bytes(ref, sem):
        pltpu.make_async_copy(ref, ref, sem).wait()

    half = FT // 2
    lanes = (pl.ds(0, half), pl.ds(half, half))

    def slot(a, h, p, q):
        spot = q * 4 + p if h == 0 else p * 4 + q
        return full.at[a * 16 + spot, :, lanes[h]]

    near = ((z, zr, zl, zo), (y, yr, yl, yo))
    own = (y, z)
    first = (dev_z, dev_y)
    second = (dev_y, dev_z)

    def spread_to(ref, devs, recv=None):
        return [send(ref, ref, dev, 0, recv) for dev in devs]

    def gather_one(a):
        return [spread_to(slot(a, h, near[h][0], own[h]), first[h]) for h in (0, 1)]

    everything = (fresh(), fresh())

    def gather_two(a, step):
        for h in (0, 1):
            spread_to(slot(a, h, near[h][step], own[h]), second[h], everything[a])

    def fill(dense, first_row):
        def some(m, carry):
            for n in range(12):
                p = m * 12 + n
                dense[p] = wv[inv_s[first_row + (p >> 7), p & 127]]
            return carry

        lax.fori_loop(0, FB * UB // 12, some, 0)

    stage_a = [gather_one(0), None]
    gather_two(0, 0)
    stage_a[1] = gather_one(1)

    for ref, last in ((wv, CAP), (dense1, NONE), (dense2, NONE)):
        ref[last] = jnp.zeros((BLK, BLK), BF16)
    loads[0].wait()
    loads[1].wait()
    inv_v[...] = jnp.full((8, BLK), CAP, I32)
    for n, (height, width) in enumerate(((FB, UB), (UB, FB))):
        i, j = idx_v[n, 0:1, :], idx_v[n, 1:2, :]
        target = jnp.where(j < width, j * height + i, NONE)
        pos_v[n : n + 1, :] = target
        spread = jnp.broadcast_to(target, (BLK, CAP)).T
        slots = lax.broadcasted_iota(I32, (CAP, BLK), 0)
        places = lax.broadcasted_iota(I32, (CAP, BLK), 1)
        for m in range(3):
            found = jnp.where(spread == places + m * BLK, slots, CAP)
            inv_v[n * 3 + m : n * 3 + m + 1, :] = jnp.min(found, axis=0, keepdims=True)
    table = pltpu.make_async_copy(inv_v, inv_s, local_sems.at[2])
    table.start()
    places_of = pltpu.make_async_copy(pos_v, pos_s, local_sems.at[7])
    places_of.start()
    def gather_rest(a):
        for step, mirror in ((1, 1), (2, 0), (3, 2)):
            for h in (0, 1):
                stage_a[a][h][mirror].wait_recv()
            gather_two(a, step)

    gather_rest(0)
    gather_two(1, 0)
    table.wait()
    places_of.wait()
    load1.wait()
    fill(dense1, 0)
    load2.start()
    gather_rest(1)
    load2.wait()
    fill(dense2, 3)

    def gathered(a):
        wait_bytes(full.at[pl.ds(a * 16, 12)], recv_sems.at[everything[a]])

    gathered(0)

    ahead = (dev_xr, dev_xl)
    behind = (dev_xl, dev_xr)
    x_ahead = (xr, xl)
    x_behind = (xl, xr)
    flight = {}

    def tile1(u, rows, count):
        return jnp.concatenate(
            [dense1[pl.ds(j * FB + rows, count)].reshape(count * BLK, BLK) for j in range(u * UPI, (u + 1) * UPI)], axis=1
        )

    def tile2(u, columns, count):
        return jnp.concatenate(
            [dense2[pl.ds(j * UB + u * UPI, UPI)].reshape(NU, BLK) for j in range(columns, columns + count)], axis=1
        )

    def step_f(u, a):
        if a == 1 and u == 0:
            gathered(1)
        tokens = full[pl.ds(a * 16, 16)].reshape(TOK, FT)
        if a == 0:
            hidden = jnp.dot(tokens, tile1(u, 0, FB), preferred_element_type=F32)
        else:
            hidden = lax.dot_general(tokens, tile2(u, 0, FB), NT, preferred_element_type=F32)
        part[a, u] = hidden.astype(BF16).reshape(2, 4, 32, NU)
        flight["core", u, a] = send(part.at[a, u, 1 - k], ag.at[a, u, 1 - k], sib, 1)

    def step_1(u, a):
        d = (u + a) % 2
        flight["core", u, a].wait_recv()
        for where in (xo, x_behind[d], x_ahead[d], x):
            part[a, u, k, where] = add(part[a, u, k, where], ag[a, u, k, where])
        flight["m1a", u, a] = send(part.at[a, u, k, xo], m1a.at[a, u], ahead[d], 2)
        flight["last", u, a] = fresh()
        send(part.at[a, u, k, x_behind[d]], mm.at[a, u, 0], behind[d], 2, flight["last", u, a])

    def step_2(u, a):
        d = (u + a) % 2
        flight["m1a", u, a].wait_recv()
        part[a, u, k, x_ahead[d]] = add(part[a, u, k, x_ahead[d]], m1a[a, u])
        send(part.at[a, u, k, x_ahead[d]], mm.at[a, u, 1], ahead[d], 2, flight["last", u, a])

    def step_3(u, a):
        d = (u + a) % 2
        wait_bytes(mm.at[a, u], recv_sems.at[flight["last", u, a]])
        total = part[a, u, k, x].astype(F32) + mm[a, u, 0].astype(F32) + mm[a, u, 1].astype(F32)
        if a == 0:
            act, rate = gelu_pair(total)
            slope[u] = rate
            ag[a, u, k, x] = act.astype(BF16)
        else:
            ag[a, u, k, x] = (total * slope[u]).astype(BF16)
        mine = ag.at[a, u, k, x]
        flight["agd", u, a] = send(mine, mine, ahead[d], 2)
        flight["ago", u, a] = send(mine, mine, behind[d], 2)

    arrived = {}

    def count(u, a):
        arrived[u, a] = arrived.get((u, a), 0) + 1
        if arrived[u, a] == 3:
            flight["s", u, a] = send(ag.at[a, u, k], ag.at[a, u, k], sib, 1)

    def step_4(u, a):
        d = (u + a) % 2
        flight["agd", u, a].wait_recv()
        got = ag.at[a, u, k, x_behind[d]]
        flight["fwd", u, a] = send(got, got, ahead[d], 2)
        count(u, a)

    def step_5(u, a):
        flight["ago", u, a].wait_recv()
        count(u, a)

    def step_6(u, a):
        flight["fwd", u, a].wait_recv()
        count(u, a)

    def step_b(u, a):
        flight["s", u, a].wait_recv()
        width = FT // 2
        rows = FB // 2
        for n in range(2):
            here = pl.ds(n * width, width)
            units = ag[a, u].reshape(TOK, NU)
            if a == 0:
                value = jnp.dot(units, tile2(u, n * rows, rows), preferred_element_type=F32)
            else:
                value = lax.dot_general(units, tile1(u, n * rows, rows), NT, preferred_element_type=F32)
            if u > 0:
                value = value + acc[a, :, here]
            if u < ITEMS - 1:
                acc[a, :, here] = value
            else:
                po[a, :, :, :, here] = value.astype(BF16).reshape(4, 4, 16, width)

    def step_t(u, a):
        for i in range(FB):
            tok_t[pl.ds(i * BLK, BLK), :] = full[pl.ds(0, 16), :, pl.ds(i * BLK, BLK)].reshape(TOK, BLK).T

    def step_w(u, a):
        if a == 1:
            pre = ag[1, u].reshape(TOK, NU)
            value = jnp.dot(tok_t[...], pre, preferred_element_type=F32).astype(BF16)
            for c in range(UPI):
                dense1[pl.ds((u * UPI + c) * FB, FB)] = value[:, c * BLK : (c + 1) * BLK].reshape(FB, BLK, BLK)
        else:
            for i in range(UPI):
                act_t[pl.ds(i * BLK, BLK), :] = ag[0, u, :, :, :, pl.ds(i * BLK, BLK)].reshape(TOK, BLK).T
            grads = full[pl.ds(16, 16)].reshape(TOK, FT)
            value = jnp.dot(act_t[...], grads, preferred_element_type=F32).astype(BF16)
            for c in range(FB):
                dense2[pl.ds(c * UB + u * UPI, UPI)] = value[:, c * BLK : (c + 1) * BLK].reshape(UPI, BLK, BLK)

    saves = []

    def step_s(u, a):
        dense, target = ((dense2, dw2_hbm), (dense1, dw1_hbm))[a]
        for save in saves:
            save.wait()

        def some(m, carry):
            for n in range(12):
                wv[m * 12 + n] = dense[pos_s[1 - a, m * 12 + n]]
            return carry

        lax.fori_loop(0, CAP // 12, some, 0)
        save = pltpu.make_async_copy(wv.at[pl.ds(0, CAP)], target, local_sems.at[9 + a])
        save.start()
        saves.append(save)

    def piece(a, h, p, q):
        return po.at[a, p, q, :, lanes[h]] if h == 0 else po.at[a, q, p, :, lanes[h]]

    far = ((zo, zr, zl, z), (yo, yr, yl, y))
    peers = ((yr, yl, yo), (zr, zl, zo))
    peer_devs = (dev_y, dev_z)
    last_devs = ((dev_z[2], dev_z[0], dev_z[1]), (dev_y[2], dev_y[0], dev_y[1]))

    def step_c(u, a):
        for n in range(4) if u == 0 else ():
            for h in (0, 1):
                flight["c1", n, a, h] = fresh()
                for d in (2, 0, 1):
                    there = piece(a, h, peers[h][d], far[h][n])
                    send(there, c1.at[a, h, n, d], peer_devs[h][d], 3, flight["c1", n, a, h])
        for h in (0, 1) if u > 0 else ():
            if u <= 4:
                n = u - 1
                wait_bytes(c1.at[a, h, n], recv_sems.at[flight["c1", n, a, h]])
                spot = piece(a, h, own[h], far[h][n])
                total = spot[...].astype(F32)
                for d in range(3):
                    total = total + c1[a, h, n, d].astype(F32)
                spot[...] = total.astype(BF16)
                if n == 0:
                    flight["c2", a, h] = fresh()
                if n < 3:
                    send(spot, c2.at[a, h, n], last_devs[h][n], 4, flight["c2", a, h])
            else:
                total = piece(a, h, own[h], far[h][3])[...].astype(F32)
                wait_bytes(c2.at[a, h], recv_sems.at[flight["c2", a, h]])
                for n in range(3):
                    total = total + c2[a, h, n].astype(F32)
                (out_ref, gin_ref)[a][:, lanes[h]] = total.astype(BF16)

    steps = {
        "F": step_f,
        "1": step_1,
        "2": step_2,
        "3": step_3,
        "4": step_4,
        "5": step_5,
        "6": step_6,
        "B": step_b,
        "T": step_t,
        "W": step_w,
        "S": step_s,
        "C": step_c,
    }
    for line in ORDER:
        for name in line.split():
            steps[name[0]](int(name[1]), "hg".index(name[2]))

    wait_bytes(full.at[pl.ds(0, 30)], send_sems.at[0])
    wait_bytes(ag, send_sems.at[1])
    wait_bytes(ag.at[:, :, :, pl.ds(0, 3)], send_sems.at[2])
    wait_bytes(c1, send_sems.at[3])
    wait_bytes(c2, send_sems.at[4])
    saves[-1].wait()


N_SEMS = 14 + 14 * ITEMS + 20


def fused(tokens, out_grad, idx1, idx2, w1, w2):
    vmem = pl.BlockSpec(memory_space=pltpu.VMEM)
    hbm = pl.BlockSpec(memory_space=pl.ANY)
    flops = 6 * 2 * TOK * FT * UT
    return pl.pallas_call(
        fused_kernel,
        out_shape=(
            jax.ShapeDtypeStruct((16, FT), BF16),
            jax.ShapeDtypeStruct((16, FT), BF16),
            jax.ShapeDtypeStruct((CAP, BLK, BLK), BF16),
            jax.ShapeDtypeStruct((CAP, BLK, BLK), BF16),
        ),
        in_specs=[pl.BlockSpec(memory_space=pltpu.HBM)] * 6,
        out_specs=(vmem, vmem, hbm, hbm),
        scratch_shapes=[
            pltpu.VMEM((CAP + 1, BLK, BLK), BF16),
            pltpu.VMEM((NONE + 1, BLK, BLK), BF16),
            pltpu.VMEM((NONE + 1, BLK, BLK), BF16),
            pltpu.VMEM((32, 16, FT), BF16),
            pltpu.VMEM((2, ITEMS, 2, 4, 32, NU), BF16),
            pltpu.VMEM((2, ITEMS, 32, NU), BF16),
            pltpu.VMEM((2, ITEMS, 2, 32, NU), BF16),
            pltpu.VMEM((ITEMS, 32, NU), F32),
            pltpu.VMEM((2, ITEMS, 2, 4, 32, NU), BF16),
            pltpu.VMEM((2, TOK, FT), F32),
            pltpu.VMEM((2, 4, 4, 16, FT), BF16),
            pltpu.VMEM((2, 2, 4, 3, 16, FT // 2), BF16),
            pltpu.VMEM((2, 2, 3, 16, FT // 2), BF16),
            pltpu.VMEM((FT, TOK), BF16),
            pltpu.VMEM((NU, TOK), BF16),
            pltpu.VMEM((2, 2, CAP), I32),
            pltpu.VMEM((2, CAP), I32),
            pltpu.SMEM((2, CAP), I32),
            pltpu.VMEM((8, BLK), I32),
            pltpu.SMEM((8, BLK), I32),
            pltpu.SemaphoreType.DMA((5,)),
            pltpu.SemaphoreType.DMA((N_SEMS,)),
            pltpu.SemaphoreType.DMA((11,)),
        ],
        compiler_params=pltpu.CompilerParams(
            collective_id=0, has_side_effects=True, vmem_limit_bytes=42 * 1024 * 1024
        ),
        cost_estimate=pl.CostEstimate(flops=flops, bytes_accessed=31_000_000, transcendentals=200_000),
        name="ffn_fused",
    )(tokens, out_grad, idx1, idx2, w1, w2)


def place_kernel(dw1, dw2, out_in, gin_in, gw1, gw2, out, gin, sems):
    copies = [
        pltpu.make_async_copy(source, target, sems.at[n])
        for n, (source, target) in enumerate(((dw1, gw1), (dw2, gw2), (out_in, out), (gin_in, gin)))
    ]
    for copy in copies:
        copy.start()
    for copy in copies:
        copy.wait()


def place(dw1, dw2, out, gin):
    hbm = pl.BlockSpec(memory_space=pl.ANY)
    shape = jax.ShapeDtypeStruct((CAP, BLK, BLK), BF16)
    small = jax.ShapeDtypeStruct((16, FT), BF16)
    return pl.pallas_call(
        place_kernel,
        out_shape=(shape, shape, small, small),
        in_specs=[hbm, hbm, hbm, hbm],
        out_specs=(hbm, hbm, hbm, hbm),
        scratch_shapes=[pltpu.SemaphoreType.DMA((4,))],
        compiler_params=pltpu.CompilerParams(vmem_limit_bytes=2 * 1024 * 1024),
        cost_estimate=pl.CostEstimate(flops=0, bytes_accessed=24_000_000, transcendentals=0),
        name="ffn_place",
    )(dw1, dw2, out, gin)


def body(tokens, out_grad, w1_blocks, w1_index, w2_blocks, w2_index):
    idx1, idx2 = w1_index.T, w2_index.T
    tokens, out_grad, idx1, idx2 = [
        pltpu.with_memory_space_constraint(value, pltpu.HBM) for value in (tokens, out_grad, idx1, idx2)
    ]
    output, grad_input, dw1, dw2 = fused(tokens, out_grad, idx1, idx2, w1_blocks, w2_blocks)
    grad_one, grad_two, output, grad_input = place(dw1, dw2, output, grad_input)
    return output, grad_input, grad_one, grad_two


def solution(mesh):
    return jax.shard_map(
        body,
        mesh=mesh,
        in_specs=(
            P("row", "col"),
            P("row", "col"),
            P(("row", "col"), None, None),
            P(("row", "col"), None),
            P(("row", "col"), None, None),
            P(("row", "col"), None),
        ),
        out_specs=(
            P("row", "col"),
            P("row", "col"),
            P(("row", "col"), None, None),
            P(("row", "col"), None, None),
        ),
        check_vma=False,
    )
```

```python
import jax
import jax.numpy as jnp
from jax import lax
from jax.experimental import pallas as pl
from jax.experimental.pallas import tpu as pltpu
from jax.sharding import PartitionSpec as P

MESH = pl.DeviceIdType.MESH
BLK = 128
CAP = 180
FB = 12
UB = 24
FT = FB * BLK
UT = UB * BLK
TOK = 256
ITEMS = 6
NU = UT // ITEMS
UPI = UB // ITEMS
PER = UPI * FB
F32 = jnp.float32
BF16 = jnp.bfloat16
I32 = jnp.int32
NONE = FB * UB
NT = (((1,), (1,)), ((), ()))

ORDER = (
    "F0h F1h F3h 10h", "F2h 11h F4h 13h", "F5h 12h 14h F2g", "15h F1g 20h 21h",
    "12g F0g 11g 22h", "23h 24h 10g 31h", "25h F4g 30h 32h", "F3g 34h 14g 13g",
    "51h T0h 40h 33h", "41h 20g F5g 42h", "21g 15g 44h 50h", "35h 22g 23g 54h",
    "43h 60h 61h 53h", "24g B0h 30g 52h", "W0h 62h 45h 31g", "25g B1h 32g 64h",
    "63h B2h 33g 34g", "W2h B3h 55h 65h", "40g 41g B4h 51g", "35g W3h 42g B5h",
    "43g C0h 44g 50g", "61g 60g W5h W4h", "45g 54g 52g W1h", "53g 62g 55g B0g",
    "63g B1g C1h 64g", "B2g 65g B3g B4g", "B5g C0g C2h S0h", "W3g W1g W5g W2g",
    "W4g C1g W0g C3h", "S0g C2g C3g C4h", "C4g C5h C5g",
)


def gelu_pair(value):
    cubic_term = 0.044715 * value * value * value
    tangent = jnp.tanh(0.7978845608 * (value + cubic_term))
    result = 0.5 * value * (1.0 + tangent)
    derivative = 0.5 * (1.0 + tangent) + 0.5 * value * (1.0 - tangent * tangent) * 0.7978845608 * (
        1.0 + 3.0 * 0.044715 * value * value
    )
    return (result, derivative)


def add(a, b):
    return (a.astype(F32) + b.astype(F32)).astype(BF16)


def fused_kernel(
    tok_hbm,
    grad_hbm,
    idx1_hbm,
    idx2_hbm,
    w1_hbm,
    w2_hbm,
    out_ref,
    gin_ref,
    dw1_hbm,
    dw2_hbm,
    wv,
    dense1,
    dense2,
    full,
    part,
    m1a,
    mm,
    slope,
    ag,
    acc,
    po,
    c1,
    c2,
    tok_t,
    act_t,
    idx_v,
    pos_v,
    pos_s,
    inv_v,
    inv_s,
    send_sems,
    recv_sems,
    local_sems,
):
    row = lax.axis_index("row")
    col = lax.axis_index("col")
    y, z = row // 4, row % 4
    x, k = col // 2, col % 2
    yr, yl, yo = (y + 1) % 4, (y + 3) % 4, (y + 2) % 4
    zr, zl, zo = (z + 1) % 4, (z + 3) % 4, (z + 2) % 4
    xr, xl, xo = (x + 1) % 4, (x + 3) % 4, (x + 2) % 4
    sib = (row, x * 2 + 1 - k)
    dev_xr, dev_xl = (row, xr * 2 + k), (row, xl * 2 + k)
    dev_y = tuple((p * 4 + z, col) for p in (yr, yl, yo))
    dev_z = tuple((y * 4 + p, col) for p in (zr, zl, zo))

    load1 = pltpu.make_async_copy(w1_hbm, wv.at[pl.ds(0, CAP)], local_sems.at[0])
    load2 = pltpu.make_async_copy(w2_hbm, wv.at[pl.ds(0, CAP)], local_sems.at[1])
    loads = [
        pltpu.make_async_copy(source, target, local_sems.at[3 + n])
        for n, (source, target) in enumerate(
            (
                (idx1_hbm, idx_v.at[0]),
                (idx2_hbm, idx_v.at[1]),
                (tok_hbm, full.at[y * 4 + z]),
                (grad_hbm, full.at[16 + y * 4 + z]),
            )
        )
    ]
    for load in loads:
        load.start()
    load1.start()

    barrier = pltpu.get_barrier_semaphore()
    for dev in (sib, dev_xr, dev_xl) + dev_y + dev_z:
        pl.semaphore_signal(barrier, inc=1, device_id=dev, device_id_type=MESH)

    for load in loads[2:]:
        load.wait()
    pl.semaphore_wait(barrier, 9)

    used = [0]

    def fresh():
        used[0] += 1
        return used[0] - 1

    def send(src, dst, dev, group, recv=None):
        copy = pltpu.make_async_remote_copy(
            src_ref=src,
            dst_ref=dst,
            send_sem=send_sems.at[group],
            recv_sem=recv_sems.at[fresh() if recv is None else recv],
            device_id=dev,
            device_id_type=MESH,
        )
        copy.start()
        return copy

    def wait_bytes(ref, sem):
        pltpu.make_async_copy(ref, ref, sem).wait()

    half = FT // 2
    lanes = (pl.ds(0, half), pl.ds(half, half))

    def slot(a, h, p, q):
        spot = q * 4 + p if h == 0 else p * 4 + q
        return full.at[a * 16 + spot, :, lanes[h]]

    near = ((z, zr, zl, zo), (y, yr, yl, yo))
    own = (y, z)
    first = (dev_z, dev_y)
    second = (dev_y, dev_z)

    def spread_to(ref, devs, recv=None):
        return [send(ref, ref, dev, 0, recv) for dev in devs]

    def gather_one(a):
        return [spread_to(slot(a, h, near[h][0], own[h]), first[h]) for h in (0, 1)]

    everything = (fresh(), fresh())

    def gather_two(a, step):
        for h in (0, 1):
            spread_to(slot(a, h, near[h][step], own[h]), second[h], everything[a])

    def fill(dense, first_row):
        def some(m, carry):
            for n in range(12):
                p = m * 12 + n
                dense[p] = wv[inv_s[first_row + (p >> 7), p & 127]]
            return carry

        lax.fori_loop(0, FB * UB // 12, some, 0)

    stage_a = [gather_one(0), None]
    gather_two(0, 0)
    stage_a[1] = gather_one(1)

    for ref, last in ((wv, CAP), (dense1, NONE), (dense2, NONE)):
        ref[last] = jnp.zeros((BLK, BLK), BF16)
    loads[0].wait()
    loads[1].wait()
    inv_v[...] = jnp.full((8, BLK), CAP, I32)
    for n, (height, width) in enumerate(((FB, UB), (UB, FB))):
        i, j = idx_v[n, 0:1, :], idx_v[n, 1:2, :]
        target = jnp.where(j < width, j * height + i, NONE)
        pos_v[n : n + 1, :] = target
        spread = jnp.broadcast_to(target, (BLK, CAP)).T
        slots = lax.broadcasted_iota(I32, (CAP, BLK), 0)
        places = lax.broadcasted_iota(I32, (CAP, BLK), 1)
        for m in range(3):
            found = jnp.where(spread == places + m * BLK, slots, CAP)
            inv_v[n * 3 + m : n * 3 + m + 1, :] = jnp.min(found, axis=0, keepdims=True)
    table = pltpu.make_async_copy(inv_v, inv_s, local_sems.at[2])
    table.start()
    places_of = pltpu.make_async_copy(pos_v, pos_s, local_sems.at[7])
    places_of.start()
    def gather_rest(a):
        for step, mirror in ((1, 1), (2, 0), (3, 2)):
            for h in (0, 1):
                stage_a[a][h][mirror].wait_recv()
            gather_two(a, step)

    gather_rest(0)
    gather_two(1, 0)
    table.wait()
    places_of.wait()
    load1.wait()
    fill(dense1, 0)
    load2.start()
    gather_rest(1)
    load2.wait()
    fill(dense2, 3)

    def gathered(a):
        wait_bytes(full.at[pl.ds(a * 16, 12)], recv_sems.at[everything[a]])

    gathered(0)

    ahead = (dev_xr, dev_xl)
    behind = (dev_xl, dev_xr)
    x_ahead = (xr, xl)
    x_behind = (xl, xr)
    flight = {}
    ready = []

    def tile1(u, rows, count):
        return jnp.concatenate(
            [dense1[pl.ds(j * FB + rows, count)].reshape(count * BLK, BLK) for j in range(u * UPI, (u + 1) * UPI)], axis=1
        )

    def tile2(u, columns, count):
        return jnp.concatenate(
            [dense2[pl.ds(j * UB + u * UPI, UPI)].reshape(NU, BLK) for j in range(columns, columns + count)], axis=1
        )

    def step_f(u, a):
        if a == 1 and not ready:
            gathered(1)
            ready.append(u)
        tokens = full[pl.ds(a * 16, 16)].reshape(TOK, FT)
        if a == 0:
            hidden = jnp.dot(tokens, tile1(u, 0, FB), preferred_element_type=F32)
        else:
            hidden = lax.dot_general(tokens, tile2(u, 0, FB), NT, preferred_element_type=F32)
        part[a, u] = hidden.astype(BF16).reshape(2, 4, 32, NU)
        flight["core", u, a] = send(part.at[a, u, 1 - k], ag.at[a, u, 1 - k], sib, 1)

    def step_1(u, a):
        d = (u + a) % 2
        flight["core", u, a].wait_recv()
        for where in (xo, x_behind[d], x_ahead[d], x):
            part[a, u, k, where] = add(part[a, u, k, where], ag[a, u, k, where])
        flight["m1a", u, a] = send(part.at[a, u, k, xo], m1a.at[a, u], ahead[d], 2)
        flight["last", u, a] = fresh()
        send(part.at[a, u, k, x_behind[d]], mm.at[a, u, 0], behind[d], 2, flight["last", u, a])

    def step_2(u, a):
        d = (u + a) % 2
        flight["m1a", u, a].wait_recv()
        part[a, u, k, x_ahead[d]] = add(part[a, u, k, x_ahead[d]], m1a[a, u])
        send(part.at[a, u, k, x_ahead[d]], mm.at[a, u, 1], ahead[d], 2, flight["last", u, a])

    def step_3(u, a):
        d = (u + a) % 2
        wait_bytes(mm.at[a, u], recv_sems.at[flight["last", u, a]])
        total = part[a, u, k, x].astype(F32) + mm[a, u, 0].astype(F32) + mm[a, u, 1].astype(F32)
        if a == 0:
            act, rate = gelu_pair(total)
            slope[u] = rate
            ag[a, u, k, x] = act.astype(BF16)
        else:
            ag[a, u, k, x] = (total * slope[u]).astype(BF16)
        mine = ag.at[a, u, k, x]
        flight["agd", u, a] = send(mine, mine, ahead[d], 2)
        flight["ago", u, a] = send(mine, mine, behind[d], 2)

    arrived = {}

    def count(u, a):
        arrived[u, a] = arrived.get((u, a), 0) + 1
        if arrived[u, a] == 3:
            flight["s", u, a] = send(ag.at[a, u, k], ag.at[a, u, k], sib, 1)

    def step_4(u, a):
        d = (u + a) % 2
        flight["agd", u, a].wait_recv()
        got = ag.at[a, u, k, x_behind[d]]
        flight["fwd", u, a] = send(got, got, ahead[d], 2)
        count(u, a)

    def step_5(u, a):
        flight["ago", u, a].wait_recv()
        count(u, a)

    def step_6(u, a):
        flight["fwd", u, a].wait_recv()
        count(u, a)

    def step_b(u, a):
        flight["s", u, a].wait_recv()
        width = FT // 2
        rows = FB // 2
        for n in range(2):
            here = pl.ds(n * width, width)
            units = ag[a, u].reshape(TOK, NU)
            if a == 0:
                value = jnp.dot(units, tile2(u, n * rows, rows), preferred_element_type=F32)
            else:
                value = lax.dot_general(units, tile1(u, n * rows, rows), NT, preferred_element_type=F32)
            if u > 0:
                value = value + acc[a, :, here]
            if u < ITEMS - 1:
                acc[a, :, here] = value
            else:
                po[a, :, :, :, here] = value.astype(BF16).reshape(4, 4, 16, width)

    def step_t(u, a):
        for i in range(FB):
            tok_t[pl.ds(i * BLK, BLK), :] = full[pl.ds(0, 16), :, pl.ds(i * BLK, BLK)].reshape(TOK, BLK).T

    def step_w(u, a):
        if a == 1:
            pre = ag[1, u].reshape(TOK, NU)
            value = jnp.dot(tok_t[...], pre, preferred_element_type=F32).astype(BF16)
            for c in range(UPI):
                dense1[pl.ds((u * UPI + c) * FB, FB)] = value[:, c * BLK : (c + 1) * BLK].reshape(FB, BLK, BLK)
        else:
            for i in range(UPI):
                act_t[pl.ds(i * BLK, BLK), :] = ag[0, u, :, :, :, pl.ds(i * BLK, BLK)].reshape(TOK, BLK).T
            grads = full[pl.ds(16, 16)].reshape(TOK, FT)
            value = jnp.dot(act_t[...], grads, preferred_element_type=F32).astype(BF16)
            for c in range(FB):
                dense2[pl.ds(c * UB + u * UPI, UPI)] = value[:, c * BLK : (c + 1) * BLK].reshape(UPI, BLK, BLK)

    saves = []

    def step_s(u, a):
        dense, target = ((dense2, dw2_hbm), (dense1, dw1_hbm))[a]
        for save in saves:
            save.wait()

        def some(m, carry):
            for n in range(12):
                wv[m * 12 + n] = dense[pos_s[1 - a, m * 12 + n]]
            return carry

        lax.fori_loop(0, CAP // 12, some, 0)
        save = pltpu.make_async_copy(wv.at[pl.ds(0, CAP)], target, local_sems.at[9 + a])
        save.start()
        saves.append(save)

    def piece(a, h, p, q):
        return po.at[a, p, q, :, lanes[h]] if h == 0 else po.at[a, q, p, :, lanes[h]]

    far = ((zo, zr, zl, z), (yo, yr, yl, y))
    peers = ((yr, yl, yo), (zr, zl, zo))
    peer_devs = (dev_y, dev_z)
    last_devs = ((dev_z[2], dev_z[0], dev_z[1]), (dev_y[2], dev_y[0], dev_y[1]))

    def step_c(u, a):
        for n in range(4) if u == 0 else ():
            for h in (0, 1):
                flight["c1", n, a, h] = fresh()
                for d in (2, 0, 1):
                    there = piece(a, h, peers[h][d], far[h][n])
                    send(there, c1.at[a, h, n, d], peer_devs[h][d], 3, flight["c1", n, a, h])
        for h in (0, 1) if u > 0 else ():
            if u <= 4:
                n = u - 1
                wait_bytes(c1.at[a, h, n], recv_sems.at[flight["c1", n, a, h]])
                spot = piece(a, h, own[h], far[h][n])
                total = spot[...].astype(F32)
                for d in range(3):
                    total = total + c1[a, h, n, d].astype(F32)
                spot[...] = total.astype(BF16)
                if n == 0:
                    flight["c2", a, h] = fresh()
                if n < 3:
                    send(spot, c2.at[a, h, n], last_devs[h][n], 4, flight["c2", a, h])
            else:
                total = piece(a, h, own[h], far[h][3])[...].astype(F32)
                wait_bytes(c2.at[a, h], recv_sems.at[flight["c2", a, h]])
                for n in range(3):
                    total = total + c2[a, h, n].astype(F32)
                (out_ref, gin_ref)[a][:, lanes[h]] = total.astype(BF16)

    steps = {
        "F": step_f,
        "1": step_1,
        "2": step_2,
        "3": step_3,
        "4": step_4,
        "5": step_5,
        "6": step_6,
        "B": step_b,
        "T": step_t,
        "W": step_w,
        "S": step_s,
        "C": step_c,
    }
    for line in ORDER:
        for name in line.split():
            steps[name[0]](int(name[1]), "hg".index(name[2]))

    wait_bytes(full.at[pl.ds(0, 30)], send_sems.at[0])
    wait_bytes(ag, send_sems.at[1])
    wait_bytes(ag.at[:, :, :, pl.ds(0, 3)], send_sems.at[2])
    wait_bytes(c1, send_sems.at[3])
    wait_bytes(c2, send_sems.at[4])
    saves[-1].wait()


N_SEMS = 14 + 14 * ITEMS + 20


def fused(tokens, out_grad, idx1, idx2, w1, w2):
    vmem = pl.BlockSpec(memory_space=pltpu.VMEM)
    hbm = pl.BlockSpec(memory_space=pl.ANY)
    flops = 6 * 2 * TOK * FT * UT
    return pl.pallas_call(
        fused_kernel,
        out_shape=(
            jax.ShapeDtypeStruct((16, FT), BF16),
            jax.ShapeDtypeStruct((16, FT), BF16),
            jax.ShapeDtypeStruct((CAP, BLK, BLK), BF16),
            jax.ShapeDtypeStruct((CAP, BLK, BLK), BF16),
        ),
        in_specs=[pl.BlockSpec(memory_space=pltpu.HBM)] * 6,
        out_specs=(vmem, vmem, hbm, hbm),
        scratch_shapes=[
            pltpu.VMEM((CAP + 1, BLK, BLK), BF16),
            pltpu.VMEM((NONE + 1, BLK, BLK), BF16),
            pltpu.VMEM((NONE + 1, BLK, BLK), BF16),
            pltpu.VMEM((32, 16, FT), BF16),
            pltpu.VMEM((2, ITEMS, 2, 4, 32, NU), BF16),
            pltpu.VMEM((2, ITEMS, 32, NU), BF16),
            pltpu.VMEM((2, ITEMS, 2, 32, NU), BF16),
            pltpu.VMEM((ITEMS, 32, NU), F32),
            pltpu.VMEM((2, ITEMS, 2, 4, 32, NU), BF16),
            pltpu.VMEM((2, TOK, FT), F32),
            pltpu.VMEM((2, 4, 4, 16, FT), BF16),
            pltpu.VMEM((2, 2, 4, 3, 16, FT // 2), BF16),
            pltpu.VMEM((2, 2, 3, 16, FT // 2), BF16),
            pltpu.VMEM((FT, TOK), BF16),
            pltpu.VMEM((NU, TOK), BF16),
            pltpu.VMEM((2, 2, CAP), I32),
            pltpu.VMEM((2, CAP), I32),
            pltpu.SMEM((2, CAP), I32),
            pltpu.VMEM((8, BLK), I32),
            pltpu.SMEM((8, BLK), I32),
            pltpu.SemaphoreType.DMA((5,)),
            pltpu.SemaphoreType.DMA((N_SEMS,)),
            pltpu.SemaphoreType.DMA((11,)),
        ],
        compiler_params=pltpu.CompilerParams(
            collective_id=0, has_side_effects=True, vmem_limit_bytes=42 * 1024 * 1024
        ),
        cost_estimate=pl.CostEstimate(flops=flops, bytes_accessed=31_000_000, transcendentals=200_000),
        name="ffn_fused",
    )(tokens, out_grad, idx1, idx2, w1, w2)


def place_kernel(dw1, dw2, out_in, gin_in, gw1, gw2, out, gin, sems):
    copies = [
        pltpu.make_async_copy(source, target, sems.at[n])
        for n, (source, target) in enumerate(((dw1, gw1), (dw2, gw2), (out_in, out), (gin_in, gin)))
    ]
    for copy in copies:
        copy.start()
    for copy in copies:
        copy.wait()


def place(dw1, dw2, out, gin):
    hbm = pl.BlockSpec(memory_space=pl.ANY)
    shape = jax.ShapeDtypeStruct((CAP, BLK, BLK), BF16)
    small = jax.ShapeDtypeStruct((16, FT), BF16)
    return pl.pallas_call(
        place_kernel,
        out_shape=(shape, shape, small, small),
        in_specs=[hbm, hbm, hbm, hbm],
        out_specs=(hbm, hbm, hbm, hbm),
        scratch_shapes=[pltpu.SemaphoreType.DMA((4,))],
        compiler_params=pltpu.CompilerParams(vmem_limit_bytes=2 * 1024 * 1024),
        cost_estimate=pl.CostEstimate(flops=0, bytes_accessed=24_000_000, transcendentals=0),
        name="ffn_place",
    )(dw1, dw2, out, gin)


def body(tokens, out_grad, w1_blocks, w1_index, w2_blocks, w2_index):
    idx1, idx2 = w1_index.T, w2_index.T
    tokens, out_grad, idx1, idx2 = [
        pltpu.with_memory_space_constraint(value, pltpu.HBM) for value in (tokens, out_grad, idx1, idx2)
    ]
    output, grad_input, dw1, dw2 = fused(tokens, out_grad, idx1, idx2, w1_blocks, w2_blocks)
    grad_one, grad_two, output, grad_input = place(dw1, dw2, output, grad_input)
    return output, grad_input, grad_one, grad_two


def solution(mesh):
    return jax.shard_map(
        body,
        mesh=mesh,
        in_specs=(
            P("row", "col"),
            P("row", "col"),
            P(("row", "col"), None, None),
            P(("row", "col"), None),
            P(("row", "col"), None, None),
            P(("row", "col"), None),
        ),
        out_specs=(
            P("row", "col"),
            P("row", "col"),
            P(("row", "col"), None, None),
            P(("row", "col"), None, None),
        ),
        check_vma=False,
    )
```

```python
import jax
import jax.numpy as jnp
from jax import lax
from jax.experimental import pallas as pl
from jax.experimental.pallas import tpu as pltpu
from jax.sharding import PartitionSpec as P

MESH = pl.DeviceIdType.MESH
BLK = 128
CAP = 180
FB = 12
UB = 24
FT = FB * BLK
UT = UB * BLK
TOK = 256
ITEMS = 6
NU = UT // ITEMS
UPI = UB // ITEMS
PER = UPI * FB
F32 = jnp.float32
BF16 = jnp.bfloat16
I32 = jnp.int32
NONE = FB * UB
NT = (((1,), (1,)), ((), ()))

ORDER = (
    "F0h F1h F3h 10h", "F2h 11h F4h 13h", "F5h 12h 14h F2g", "15h F1g 20h 21h",
    "12g F0g 11g 22h", "23h 24h 10g 31h", "25h F4g 30h 32h", "F3g 34h 14g 13g",
    "51h T0h 40h 33h", "41h 20g F5g 42h", "21g 15g 44h 50h", "35h 22g 23g 54h",
    "43h 60h 61h 53h", "24g B0h 30g 52h", "W0h 62h 45h 31g", "25g B1h 32g 64h",
    "63h B2h 33g 34g", "W2h B3h 55h 65h", "40g 41g B4h 51g", "35g W3h 42g B5h",
    "43g C0h 44g 50g", "61g 60g W5h W4h", "45g 54g 52g W1h", "53g 62g 55g B0g",
    "63g B1g C1h 64g", "B2g 65g B3g B4g", "B5g C0g C2h S0h", "W3g W1g W5g W2g",
    "W4g C1g W0g C3h", "S0g C2g C3g C4h", "C4g C5h C5g",
)


def gelu_pair(value):
    cubic_term = 0.044715 * value * value * value
    tangent = jnp.tanh(0.7978845608 * (value + cubic_term))
    result = 0.5 * value * (1.0 + tangent)
    derivative = 0.5 * (1.0 + tangent) + 0.5 * value * (1.0 - tangent * tangent) * 0.7978845608 * (
        1.0 + 3.0 * 0.044715 * value * value
    )
    return (result, derivative)


def add(a, b):
    return (a.astype(F32) + b.astype(F32)).astype(BF16)


def fused_kernel(
    tok_hbm,
    grad_hbm,
    idx1_hbm,
    idx2_hbm,
    w1_hbm,
    w2_hbm,
    out_ref,
    gin_ref,
    dw1_hbm,
    dw2_hbm,
    wv,
    dense1,
    dense2,
    full,
    part,
    m1a,
    mm,
    slope,
    ag,
    acc,
    po,
    c1,
    c2,
    tok_t,
    act_t,
    idx_v,
    pos_v,
    pos_s,
    inv_v,
    inv_s,
    send_sems,
    recv_sems,
    local_sems,
):
    row = lax.axis_index("row")
    col = lax.axis_index("col")
    y, z = row // 4, row % 4
    x, k = col // 2, col % 2
    yr, yl, yo = (y + 1) % 4, (y + 3) % 4, (y + 2) % 4
    zr, zl, zo = (z + 1) % 4, (z + 3) % 4, (z + 2) % 4
    xr, xl, xo = (x + 1) % 4, (x + 3) % 4, (x + 2) % 4
    sib = (row, x * 2 + 1 - k)
    dev_xr, dev_xl = (row, xr * 2 + k), (row, xl * 2 + k)
    dev_y = tuple((p * 4 + z, col) for p in (yr, yl, yo))
    dev_z = tuple((y * 4 + p, col) for p in (zr, zl, zo))

    load1 = pltpu.make_async_copy(w1_hbm, wv.at[pl.ds(0, CAP)], local_sems.at[0])
    load2 = pltpu.make_async_copy(w2_hbm, wv.at[pl.ds(0, CAP)], local_sems.at[1])
    loads = [
        pltpu.make_async_copy(source, target, local_sems.at[3 + n])
        for n, (source, target) in enumerate(
            (
                (idx1_hbm, idx_v.at[0]),
                (idx2_hbm, idx_v.at[1]),
                (tok_hbm, full.at[y * 4 + z]),
                (grad_hbm, full.at[16 + y * 4 + z]),
            )
        )
    ]
    for load in loads:
        load.start()
    load1.start()

    barrier = pltpu.get_barrier_semaphore()
    for dev in (sib, dev_xr, dev_xl) + dev_y + dev_z:
        pl.semaphore_signal(barrier, inc=1, device_id=dev, device_id_type=MESH)

    for load in loads[2:]:
        load.wait()
    pl.semaphore_wait(barrier, 9)

    used = [0]

    def fresh():
        used[0] += 1
        return used[0] - 1

    def send(src, dst, dev, group, recv=None):
        copy = pltpu.make_async_remote_copy(
            src_ref=src,
            dst_ref=dst,
            send_sem=send_sems.at[group],
            recv_sem=recv_sems.at[fresh() if recv is None else recv],
            device_id=dev,
            device_id_type=MESH,
        )
        copy.start()
        return copy

    def wait_bytes(ref, sem):
        pltpu.make_async_copy(ref, ref, sem).wait()

    half = FT // 2
    lanes = (pl.ds(0, half), pl.ds(half, half))

    def slot(a, h, p, q):
        spot = q * 4 + p if h == 0 else p * 4 + q
        return full.at[a * 16 + spot, :, lanes[h]]

    near = ((z, zr, zl, zo), (y, yr, yl, yo))
    own = (y, z)
    first = (dev_z, dev_y)
    second = (dev_y, dev_z)

    def spread_to(ref, devs, recv=None):
        return [send(ref, ref, dev, 0, recv) for dev in devs]

    def gather_one(a):
        recvs = [fresh() for _ in range(3)]
        for h in (0, 1):
            for dev, recv in zip(first[h], recvs):
                spread_to(slot(a, h, near[h][0], own[h]), (dev,), recv)
        return recvs

    everything = (fresh(), fresh())

    def gather_two(a, step):
        for h in (0, 1):
            spread_to(slot(a, h, near[h][step], own[h]), second[h], everything[a])

    def fill(dense, first_row):
        def some(m, carry):
            for n in range(12):
                p = m * 12 + n
                dense[p] = wv[inv_s[first_row + (p >> 7), p & 127]]
            return carry

        lax.fori_loop(0, FB * UB // 12, some, 0)

    stage_a = [gather_one(0), None]
    gather_two(0, 0)
    stage_a[1] = gather_one(1)

    for ref, last in ((wv, CAP), (dense1, NONE), (dense2, NONE)):
        ref[last] = jnp.zeros((BLK, BLK), BF16)
    loads[0].wait()
    loads[1].wait()
    inv_v[...] = jnp.full((8, BLK), CAP, I32)
    for n, (height, width) in enumerate(((FB, UB), (UB, FB))):
        i, j = idx_v[n, 0:1, :], idx_v[n, 1:2, :]
        target = jnp.where(j < width, j * height + i, NONE)
        pos_v[n : n + 1, :] = target
        spread = jnp.broadcast_to(target, (BLK, CAP)).T
        slots = lax.broadcasted_iota(I32, (CAP, BLK), 0)
        places = lax.broadcasted_iota(I32, (CAP, BLK), 1)
        for m in range(3):
            found = jnp.where(spread == places + m * BLK, slots, CAP)
            inv_v[n * 3 + m : n * 3 + m + 1, :] = jnp.min(found, axis=0, keepdims=True)
    table = pltpu.make_async_copy(inv_v, inv_s, local_sems.at[2])
    table.start()
    places_of = pltpu.make_async_copy(pos_v, pos_s, local_sems.at[7])
    places_of.start()
    def gather_rest(a):
        for step, mirror in ((1, 1), (2, 0), (3, 2)):
            wait_bytes(full.at[0], recv_sems.at[stage_a[a][mirror]])
            gather_two(a, step)

    gather_rest(0)
    gather_two(1, 0)
    table.wait()
    places_of.wait()
    load1.wait()
    fill(dense1, 0)
    load2.start()
    gather_rest(1)
    load2.wait()
    fill(dense2, 3)

    def gathered(a):
        wait_bytes(full.at[pl.ds(a * 16, 12)], recv_sems.at[everything[a]])

    gathered(0)

    ahead = (dev_xr, dev_xl)
    behind = (dev_xl, dev_xr)
    x_ahead = (xr, xl)
    x_behind = (xl, xr)
    flight = {}
    ready = []

    def tile1(u, rows, count):
        return jnp.concatenate(
            [dense1[pl.ds(j * FB + rows, count)].reshape(count * BLK, BLK) for j in range(u * UPI, (u + 1) * UPI)], axis=1
        )

    def tile2(u, columns, count):
        return jnp.concatenate(
            [dense2[pl.ds(j * UB + u * UPI, UPI)].reshape(NU, BLK) for j in range(columns, columns + count)], axis=1
        )

    def step_f(u, a):
        if a == 1 and not ready:
            gathered(1)
            ready.append(u)
        tokens = full[pl.ds(a * 16, 16)].reshape(TOK, FT)
        if a == 0:
            hidden = jnp.dot(tokens, tile1(u, 0, FB), preferred_element_type=F32)
        else:
            hidden = lax.dot_general(tokens, tile2(u, 0, FB), NT, preferred_element_type=F32)
        part[a, u] = hidden.astype(BF16).reshape(2, 4, 32, NU)
        flight["sems", u, a] = (fresh(), fresh())
        flight["core", u, a] = send(part.at[a, u, 1 - k], ag.at[a, u, 1 - k], sib, 1, flight["sems", u, a][0])

    def step_1(u, a):
        d = (u + a) % 2
        flight["core", u, a].wait_recv()
        for where in (xo, x_behind[d], x_ahead[d], x):
            part[a, u, k, where] = add(part[a, u, k, where], ag[a, u, k, where])
        flight["m1a", u, a] = send(part.at[a, u, k, xo], m1a.at[a, u], ahead[d], 2, flight["sems", u, a][1])
        flight["last", u, a] = fresh()
        send(part.at[a, u, k, x_behind[d]], mm.at[a, u, 0], behind[d], 2, flight["last", u, a])

    def step_2(u, a):
        d = (u + a) % 2
        flight["m1a", u, a].wait_recv()
        part[a, u, k, x_ahead[d]] = add(part[a, u, k, x_ahead[d]], m1a[a, u])
        send(part.at[a, u, k, x_ahead[d]], mm.at[a, u, 1], ahead[d], 2, flight["last", u, a])

    def step_3(u, a):
        d = (u + a) % 2
        wait_bytes(mm.at[a, u], recv_sems.at[flight["last", u, a]])
        total = part[a, u, k, x].astype(F32) + mm[a, u, 0].astype(F32) + mm[a, u, 1].astype(F32)
        if a == 0:
            act, rate = gelu_pair(total)
            slope[u] = rate
            ag[a, u, k, x] = act.astype(BF16)
        else:
            ag[a, u, k, x] = (total * slope[u]).astype(BF16)
        mine = ag.at[a, u, k, x]
        flight["agd", u, a] = send(mine, mine, ahead[d], 2, flight["sems", u, a][0])
        flight["ago", u, a] = send(mine, mine, behind[d], 2, flight["sems", u, a][1])

    arrived = {}

    def count(u, a):
        arrived[u, a] = arrived.get((u, a), 0) + 1
        if arrived[u, a] == 3:
            flight["s", u, a] = send(ag.at[a, u, k], ag.at[a, u, k], sib, 1)

    def step_4(u, a):
        d = (u + a) % 2
        flight["agd", u, a].wait_recv()
        got = ag.at[a, u, k, x_behind[d]]
        flight["fwd", u, a] = send(got, got, ahead[d], 2)
        count(u, a)

    def step_5(u, a):
        flight["ago", u, a].wait_recv()
        count(u, a)

    def step_6(u, a):
        flight["fwd", u, a].wait_recv()
        count(u, a)

    def step_b(u, a):
        flight["s", u, a].wait_recv()
        width = FT // 2
        rows = FB // 2
        for n in range(2):
            here = pl.ds(n * width, width)
            units = ag[a, u].reshape(TOK, NU)
            if a == 0:
                value = jnp.dot(units, tile2(u, n * rows, rows), preferred_element_type=F32)
            else:
                value = lax.dot_general(units, tile1(u, n * rows, rows), NT, preferred_element_type=F32)
            if u > 0:
                value = value + acc[a, :, here]
            if u < ITEMS - 1:
                acc[a, :, here] = value
            else:
                po[a, :, :, :, here] = value.astype(BF16).reshape(4, 4, 16, width)

    def step_t(u, a):
        for i in range(FB):
            tok_t[pl.ds(i * BLK, BLK), :] = full[pl.ds(0, 16), :, pl.ds(i * BLK, BLK)].reshape(TOK, BLK).T

    def step_w(u, a):
        if a == 1:
            pre = ag[1, u].reshape(TOK, NU)
            value = jnp.dot(tok_t[...], pre, preferred_element_type=F32).astype(BF16)
            for c in range(UPI):
                dense1[pl.ds((u * UPI + c) * FB, FB)] = value[:, c * BLK : (c + 1) * BLK].reshape(FB, BLK, BLK)
        else:
            for i in range(UPI):
                act_t[pl.ds(i * BLK, BLK), :] = ag[0, u, :, :, :, pl.ds(i * BLK, BLK)].reshape(TOK, BLK).T
            grads = full[pl.ds(16, 16)].reshape(TOK, FT)
            value = jnp.dot(act_t[...], grads, preferred_element_type=F32).astype(BF16)
            for c in range(FB):
                dense2[pl.ds(c * UB + u * UPI, UPI)] = value[:, c * BLK : (c + 1) * BLK].reshape(UPI, BLK, BLK)

    saves = []

    def step_s(u, a):
        dense, target = ((dense2, dw2_hbm), (dense1, dw1_hbm))[a]
        for save in saves:
            save.wait()

        def some(m, carry):
            for n in range(12):
                wv[m * 12 + n] = dense[pos_s[1 - a, m * 12 + n]]
            return carry

        lax.fori_loop(0, CAP // 12, some, 0)
        save = pltpu.make_async_copy(wv.at[pl.ds(0, CAP)], target, local_sems.at[9 + a])
        save.start()
        saves.append(save)

    def piece(a, h, p, q):
        return po.at[a, p, q, :, lanes[h]] if h == 0 else po.at[a, q, p, :, lanes[h]]

    far = ((zo, zr, zl, z), (yo, yr, yl, y))
    peers = ((yr, yl, yo), (zr, zl, zo))
    peer_devs = (dev_y, dev_z)
    last_devs = ((dev_z[2], dev_z[0], dev_z[1]), (dev_y[2], dev_y[0], dev_y[1]))

    def step_c(u, a):
        for n in range(4) if u == 0 else ():
            flight["c1", n, a] = fresh()
            for h in (0, 1):
                for d in (2, 0, 1):
                    there = piece(a, h, peers[h][d], far[h][n])
                    send(there, c1.at[a, n, h, d], peer_devs[h][d], 3, flight["c1", n, a])
        if 1 <= u <= 4:
            wait_bytes(c1.at[a, u - 1], recv_sems.at[flight["c1", u - 1, a]])
        if u == 1:
            flight["c2", a] = fresh()
        if u == 5:
            wait_bytes(c2.at[a], recv_sems.at[flight["c2", a]])
        for h in (0, 1) if u > 0 else ():
            if u <= 4:
                n = u - 1
                spot = piece(a, h, own[h], far[h][n])
                total = spot[...].astype(F32)
                for d in range(3):
                    total = total + c1[a, n, h, d].astype(F32)
                spot[...] = total.astype(BF16)
                if n < 3:
                    send(spot, c2.at[a, h, n], last_devs[h][n], 4, flight["c2", a])
            else:
                total = piece(a, h, own[h], far[h][3])[...].astype(F32)
                for n in range(3):
                    total = total + c2[a, h, n].astype(F32)
                (out_ref, gin_ref)[a][:, lanes[h]] = total.astype(BF16)

    steps = {
        "F": step_f,
        "1": step_1,
        "2": step_2,
        "3": step_3,
        "4": step_4,
        "5": step_5,
        "6": step_6,
        "B": step_b,
        "T": step_t,
        "W": step_w,
        "S": step_s,
        "C": step_c,
    }
    for line in ORDER:
        for name in line.split():
            steps[name[0]](int(name[1]), "hg".index(name[2]))

    wait_bytes(full.at[pl.ds(0, 30)], send_sems.at[0])
    wait_bytes(ag, send_sems.at[1])
    wait_bytes(ag.at[:, :, :, pl.ds(0, 3)], send_sems.at[2])
    wait_bytes(c1, send_sems.at[3])
    wait_bytes(c2, send_sems.at[4])
    saves[-1].wait()


N_SEMS = 8 + 10 * ITEMS + 10


def fused(tokens, out_grad, idx1, idx2, w1, w2):
    vmem = pl.BlockSpec(memory_space=pltpu.VMEM)
    hbm = pl.BlockSpec(memory_space=pl.ANY)
    flops = 6 * 2 * TOK * FT * UT
    return pl.pallas_call(
        fused_kernel,
        out_shape=(
            jax.ShapeDtypeStruct((16, FT), BF16),
            jax.ShapeDtypeStruct((16, FT), BF16),
            jax.ShapeDtypeStruct((CAP, BLK, BLK), BF16),
            jax.ShapeDtypeStruct((CAP, BLK, BLK), BF16),
        ),
        in_specs=[pl.BlockSpec(memory_space=pltpu.HBM)] * 6,
        out_specs=(vmem, vmem, hbm, hbm),
        scratch_shapes=[
            pltpu.VMEM((CAP + 1, BLK, BLK), BF16),
            pltpu.VMEM((NONE + 1, BLK, BLK), BF16),
            pltpu.VMEM((NONE + 1, BLK, BLK), BF16),
            pltpu.VMEM((32, 16, FT), BF16),
            pltpu.VMEM((2, ITEMS, 2, 4, 32, NU), BF16),
            pltpu.VMEM((2, ITEMS, 32, NU), BF16),
            pltpu.VMEM((2, ITEMS, 2, 32, NU), BF16),
            pltpu.VMEM((ITEMS, 32, NU), F32),
            pltpu.VMEM((2, ITEMS, 2, 4, 32, NU), BF16),
            pltpu.VMEM((2, TOK, FT), F32),
            pltpu.VMEM((2, 4, 4, 16, FT), BF16),
            pltpu.VMEM((2, 4, 2, 3, 16, FT // 2), BF16),
            pltpu.VMEM((2, 2, 3, 16, FT // 2), BF16),
            pltpu.VMEM((FT, TOK), BF16),
            pltpu.VMEM((NU, TOK), BF16),
            pltpu.VMEM((2, 2, CAP), I32),
            pltpu.VMEM((2, CAP), I32),
            pltpu.SMEM((2, CAP), I32),
            pltpu.VMEM((8, BLK), I32),
            pltpu.SMEM((8, BLK), I32),
            pltpu.SemaphoreType.DMA((5,)),
            pltpu.SemaphoreType.DMA((N_SEMS,)),
            pltpu.SemaphoreType.DMA((11,)),
        ],
        compiler_params=pltpu.CompilerParams(
            collective_id=0, has_side_effects=True, vmem_limit_bytes=42 * 1024 * 1024
        ),
        cost_estimate=pl.CostEstimate(flops=flops, bytes_accessed=31_000_000, transcendentals=200_000),
        name="ffn_fused",
    )(tokens, out_grad, idx1, idx2, w1, w2)


def place_kernel(dw1, dw2, out_in, gin_in, gw1, gw2, out, gin, sems):
    copies = [
        pltpu.make_async_copy(source, target, sems.at[n])
        for n, (source, target) in enumerate(((dw1, gw1), (dw2, gw2), (out_in, out), (gin_in, gin)))
    ]
    for copy in copies:
        copy.start()
    for copy in copies:
        copy.wait()


def place(dw1, dw2, out, gin):
    hbm = pl.BlockSpec(memory_space=pl.ANY)
    shape = jax.ShapeDtypeStruct((CAP, BLK, BLK), BF16)
    small = jax.ShapeDtypeStruct((16, FT), BF16)
    return pl.pallas_call(
        place_kernel,
        out_shape=(shape, shape, small, small),
        in_specs=[hbm, hbm, hbm, hbm],
        out_specs=(hbm, hbm, hbm, hbm),
        scratch_shapes=[pltpu.SemaphoreType.DMA((4,))],
        compiler_params=pltpu.CompilerParams(vmem_limit_bytes=2 * 1024 * 1024),
        cost_estimate=pl.CostEstimate(flops=0, bytes_accessed=24_000_000, transcendentals=0),
        name="ffn_place",
    )(dw1, dw2, out, gin)


def body(tokens, out_grad, w1_blocks, w1_index, w2_blocks, w2_index):
    idx1, idx2 = w1_index.T, w2_index.T
    tokens, out_grad, idx1, idx2 = [
        pltpu.with_memory_space_constraint(value, pltpu.HBM) for value in (tokens, out_grad, idx1, idx2)
    ]
    output, grad_input, dw1, dw2 = fused(tokens, out_grad, idx1, idx2, w1_blocks, w2_blocks)
    grad_one, grad_two, output, grad_input = place(dw1, dw2, output, grad_input)
    return output, grad_input, grad_one, grad_two


def solution(mesh):
    return jax.shard_map(
        body,
        mesh=mesh,
        in_specs=(
            P("row", "col"),
            P("row", "col"),
            P(("row", "col"), None, None),
            P(("row", "col"), None),
            P(("row", "col"), None, None),
            P(("row", "col"), None),
        ),
        out_specs=(
            P("row", "col"),
            P("row", "col"),
            P(("row", "col"), None, None),
            P(("row", "col"), None, None),
        ),
        check_vma=False,
    )
```
